32 devices in a mesh: dp: 8 (over z, x), seq: 4 (over y, core).
Axes of the slice: x: 2, y: 2, z: 4, core: 2. Of those that a mesh axis runs over, the one named last changes fastest.
Arguments:
- frames: bfloat16 [8, 1024, 1280], P('dp', 'seq'), may hold values from -6 to 6
- live: int32 [8, 1024], P('dp', 'seq'), may hold values from 0 to 1
- norm_gain: float32 [1280], replicated, may hold values from 0.25 to 1.75
- w_qkv: bfloat16 [1280, 1920], P('dp')
- w_out: bfloat16 [640, 1280], P('dp'), may hold values from -0.25 to 0.25
- cotangent: bfloat16 [8, 1024, 1280], P('dp', 'seq'), may hold values from -6 to 6
Outputs:
- grad_frames: bfloat16 [8, 1024, 1280], P('dp', 'seq')
- grad_qkv: float32 [1280, 1920], P('dp', 'seq')
- grad_out: float32 [640, 1280], P('dp', 'seq')
The draws below stay inside these ranges and needn't reach their ends.
All inputs are finite; a program needn't handle non-finite values.
Results may differ from the reference program's by a relative error of at most 0.0095.
Values may be sent and summed in bfloat16 or wider, within the bound.
A program may use at most 64 MiB of HBM per device.

```python
import math
import jax
import jax.numpy as jnp
from jax import lax

D = 1280
HEADS = 10
HEAD_DIM = 64
WIN = 512
FRAMES_DEV = 256
INNER = 640
SEQS = 8
FRAMES = 1024


def draw_live(key, part):
    level_key, frame_key = jax.random.split(key)
    run_count = FRAMES // FRAMES_DEV
    levels = jax.random.randint(level_key, (SEQS, run_count, 1), 0, 5)
    rolls = jax.random.randint(frame_key, (SEQS, run_count, FRAMES_DEV), 0, 4)
    return (rolls < levels).astype(jnp.int32).reshape(SEQS, FRAMES)


def draw_w_qkv(key, part):
    drawn = jax.random.normal(key, (D, 3 * INNER), jnp.float32) / math.sqrt(D)
    return drawn.astype(jnp.bfloat16)


def shard_levels(rng, dims, pieces, least, largest):
    def one(dim, blocks):
        draws = jax.random.uniform(jax.random.fold_in(jax.random.fold_in(rng, 6), dim), (blocks,), jnp.float32, least / len(pieces), largest / len(pieces))
        return jnp.repeat(jnp.exp(draws), dims[dim] // blocks).reshape((-1,) + (1,) * (len(dims) - dim - 1))

    level = one(*pieces[0])
    for cut in pieces[1:]:
        level = level * one(*cut)
    return level


def noise(own_key, extent, width, most, pieces=(), held_as=jnp.bfloat16):
    array = width * jax.random.normal(own_key, extent, jnp.float32)
    if pieces:
        array = array * shard_levels(own_key, extent, pieces, -0.22, 0.18)
    return jnp.clip(array, -most, most).astype(held_as)


def setup_inputs(seed: int = 0) -> dict:
    streams_of = jax.random.split(jax.random.key(seed), 7)
    return {
        "frames": noise(streams_of[0], (SEQS, FRAMES, D), 1.0, 6.0, ((0, 8), (1, 4))),
        "live": draw_live(jax.random.fold_in(streams_of[6], 71), 0),
        "norm_gain": jnp.clip(1.0 + 0.15 * jax.random.normal(streams_of[2], (D,), jnp.float32), 0.25, 1.75),
        "w_qkv": draw_w_qkv(jax.random.fold_in(streams_of[6], 71), 0),
        "w_out": noise(streams_of[4], (INNER, D), INNER ** -0.5, 0.25, ((0, 8),)),
        "cotangent": noise(streams_of[5], (SEQS, FRAMES, D), 1.0, 6.0, ((0, 8), (1, 4))),
    }


EPS = 1e-05
NEG = -1e+30

def norm_rows(values_in):
    average = lax.optimization_barrier(jnp.mean(values_in, axis=-1, keepdims=True))
    centred = values_in - average
    inverse = lax.rsqrt(lax.optimization_barrier(jnp.mean(centred * centred, axis=-1, keepdims=True)) + EPS)
    return (centred * inverse, inverse)

def block_terms(query_blk, key_blk, value_blk, grad_blk, allowed, query_live):
    length = query_blk.shape[0]
    key_span = key_blk.shape[0]
    score_scale = 1.0 / math.sqrt(HEAD_DIM)
    query_heads = query_blk.reshape(length, HEADS, HEAD_DIM).astype(jnp.float32)
    key_heads = key_blk.reshape(key_span, HEADS, HEAD_DIM).astype(jnp.float32)
    value_heads = value_blk.reshape(key_span, HEADS, HEAD_DIM).astype(jnp.float32)
    grad_heads = grad_blk.reshape(length, HEADS, HEAD_DIM).astype(jnp.float32)
    scores = jnp.einsum('bhd,shd->hbs', query_heads, key_heads) * score_scale
    scores = jnp.where(allowed[None], scores, NEG)
    row_peak = lax.optimization_barrier(jnp.max(scores, axis=-1, keepdims=True))
    exponent = jnp.exp(scores - row_peak)
    probabilities = exponent / lax.optimization_barrier(jnp.sum(exponent, axis=-1, keepdims=True))
    probs_b = lax.optimization_barrier(probabilities.astype(jnp.bfloat16)).astype(jnp.float32)
    mixed = jnp.einsum('hbs,shd->bhd', probs_b, value_heads) * query_live[:, None, None]
    attended = mixed.astype(jnp.bfloat16)
    attended_f = lax.optimization_barrier(attended).astype(jnp.float32)
    row_delta = lax.optimization_barrier(jnp.sum(grad_heads * attended_f, axis=-1))
    grad_probs = jnp.einsum('bhd,shd->hbs', grad_heads, value_heads)
    grad_scores = probabilities * (grad_probs - jnp.transpose(row_delta)[:, :, None]) * score_scale
    grad_scores = lax.optimization_barrier(grad_scores.astype(jnp.bfloat16)).astype(jnp.float32)
    grad_query = jnp.einsum('hbs,shd->bhd', grad_scores, key_heads)
    grad_key = jnp.einsum('hbs,bhd->shd', grad_scores, query_heads)
    grad_value = jnp.einsum('hbs,bhd->shd', probs_b, grad_heads)
    return (attended.reshape(length, INNER), grad_query.reshape(length, INNER), grad_key.reshape(key_span, INNER), grad_value.reshape(key_span, INNER))

def sequence_terms(query, keys, values, grad_att, live_row):
    block_rows = min(FRAMES_DEV, 512)
    block_count = FRAMES // block_rows
    key_span = block_rows + 2 * WIN
    padded_keys = jnp.pad(keys, ((WIN, WIN), (0, 0)))
    padded_values = jnp.pad(values, ((WIN, WIN), (0, 0)))
    live_float = live_row.astype(jnp.float32)
    padded_live = jnp.pad(live_float, (WIN, WIN))
    empty = jnp.zeros((FRAMES + 2 * WIN, INNER), jnp.float32)
    key_pos = jnp.arange(key_span, dtype=jnp.int32) - WIN
    query_pos = jnp.arange(block_rows, dtype=jnp.int32)
    in_window = jnp.abs(query_pos[:, None] - key_pos[None, :]) <= WIN

    def step(carry, index):
        key_grads, value_grads = carry
        first_row = (index * block_rows).astype(jnp.int32)
        query_blk = lax.dynamic_slice_in_dim(query, first_row, block_rows, 0)
        grad_blk = lax.dynamic_slice_in_dim(grad_att, first_row, block_rows, 0)
        query_live = lax.dynamic_slice_in_dim(live_float, first_row, block_rows, 0)
        key_blk = lax.dynamic_slice_in_dim(padded_keys, first_row, key_span, 0)
        value_blk = lax.dynamic_slice_in_dim(padded_values, first_row, key_span, 0)
        key_live = lax.dynamic_slice_in_dim(padded_live, first_row, key_span, 0)
        allowed = in_window & (key_live[None, :] > 0.5)
        attended, grad_query, grad_key, grad_value = block_terms(query_blk, key_blk, value_blk, grad_blk, allowed, query_live)
        key_grads = lax.dynamic_update_slice_in_dim(key_grads, lax.dynamic_slice_in_dim(key_grads, first_row, key_span, 0) + grad_key, first_row, 0)
        value_grads = lax.dynamic_update_slice_in_dim(value_grads, lax.dynamic_slice_in_dim(value_grads, first_row, key_span, 0) + grad_value, first_row, 0)
        return ((key_grads, value_grads), (attended, grad_query))
    (key_grads, value_grads), (attended, grad_query) = lax.scan(step, (empty, empty), jnp.arange(block_count, dtype=jnp.int32))
    return (attended.reshape(FRAMES, INNER), grad_query.reshape(FRAMES, INNER), key_grads[WIN:WIN + FRAMES], value_grads[WIN:WIN + FRAMES])

def reference(frames, live, norm_gain, w_qkv, w_out, cotangent):

    def one_sequence(inputs):
        frame_rows, live_row, upstream = inputs
        hidden = frame_rows.astype(jnp.float32)
        unit_rows, inverse = norm_rows(hidden)
        normed = (unit_rows * norm_gain).astype(jnp.bfloat16)
        projected = jnp.dot(normed, w_qkv, preferred_element_type=jnp.float32).astype(jnp.bfloat16)
        query = projected[:, :INNER]
        keys = projected[:, INNER:2 * INNER]
        values = projected[:, 2 * INNER:]
        live_float = live_row.astype(jnp.float32)
        grad_att = (jnp.dot(upstream, w_out.T, preferred_element_type=jnp.float32) * live_float[:, None]).astype(jnp.bfloat16)
        attended, grad_query, grad_key, grad_value = sequence_terms(query, keys, values, grad_att, live_row)
        grad_projected = jnp.concatenate([grad_query, grad_key, grad_value], axis=1).astype(jnp.bfloat16)
        term_qkv = jnp.dot(normed.T, grad_projected, preferred_element_type=jnp.float32)
        term_out = jnp.dot(attended.T, upstream, preferred_element_type=jnp.float32)
        grad_unit = jnp.dot(grad_projected, w_qkv.T, preferred_element_type=jnp.float32) * norm_gain
        through = inverse * (grad_unit - lax.optimization_barrier(jnp.mean(grad_unit, axis=-1, keepdims=True)) - unit_rows * lax.optimization_barrier(jnp.mean(grad_unit * unit_rows, axis=-1, keepdims=True)))
        grad_rows = (upstream.astype(jnp.float32) + through).astype(jnp.bfloat16)
        return (grad_rows, term_qkv, term_out)
    grad_rows, terms_qkv, terms_out = lax.map(one_sequence, (frames, live, cotangent))
    factor = 1.0 / math.sqrt(SEQS * FRAMES)
    return (grad_rows, lax.optimization_barrier(jnp.sum(terms_qkv, axis=0)) * factor, lax.optimization_barrier(jnp.sum(terms_out, axis=0)) * factor)
```

```python
import functools
import math

import jax
import jax.numpy as jnp
from jax import lax
from jax.experimental import pallas as pl
from jax.experimental.pallas import tpu as pltpu
from jax.sharding import PartitionSpec as P

HEAD_DIM = 64
WIN = 512


EPS = 1e-05
NEG = -1e30


def from_behind(value, axis, steps):
    count = lax.axis_size(axis)
    leading, last = (max(0, -steps), min(count, count - steps))
    return lax.ppermute(value, axis, [(source, source + steps) for source in range(leading, last)])


def norm_rows(values_in):
    average = jnp.mean(values_in, axis=-1, keepdims=True)
    centred = values_in - average
    inverse = lax.rsqrt(jnp.mean(centred * centred, axis=-1, keepdims=True) + EPS)
    return (centred * inverse, inverse)


def against(left, right):
    return lax.dot_general(
        left, right, (((1,), (1,)), ((), ())), preferred_element_type=jnp.float32
    )


def leading(left, right):
    return lax.dot_general(
        left, right, (((0,), (0,)), ((), ())), preferred_element_type=jnp.float32
    )


def head_terms(query_head, key_head, value_head, grad_head, allowed, query_live, score_scale):
    scores = jnp.where(allowed, against(query_head, key_head) * score_scale, NEG)
    row_peak = jnp.max(scores, axis=-1, keepdims=True)
    exponent = jnp.exp(scores - row_peak)
    probabilities = exponent / jnp.sum(exponent, axis=-1, keepdims=True)
    probs_b = probabilities.astype(jnp.bfloat16)
    mixed = jnp.dot(probs_b, value_head, preferred_element_type=jnp.float32) * query_live[:, None]
    attended = mixed.astype(jnp.bfloat16)
    row_delta = jnp.sum(grad_head.astype(jnp.float32) * attended.astype(jnp.float32), axis=1)
    grad_probs = against(grad_head, value_head)
    grad_scores = (probabilities * (grad_probs - row_delta[:, None]) * score_scale).astype(
        jnp.bfloat16
    )
    grad_query = jnp.dot(grad_scores, key_head, preferred_element_type=jnp.float32)
    grad_key = leading(grad_scores, query_head)
    grad_value = leading(probs_b, grad_head)
    return (attended, grad_query, grad_key, grad_value)


def body(frames, live, norm_gain, w_qkv, w_out, cotangent):
    length = frames.shape[1]
    n_data = lax.axis_size("dp")
    n_seq = lax.axis_size("seq")
    full_qkv, full_out = (
        lax.all_gather(w_qkv, "dp", axis=0, tiled=True),
        lax.all_gather(w_out, "dp", axis=0, tiled=True),
    )
    inner = full_out.shape[0]
    heads = inner // HEAD_DIM
    hidden = frames[0].astype(jnp.float32)
    unit_rows, inverse = norm_rows(hidden)
    normed = (unit_rows * norm_gain).astype(jnp.bfloat16)
    projected = jnp.dot(normed, full_qkv, preferred_element_type=jnp.float32).astype(jnp.bfloat16)
    query = projected[:, :inner]
    key_values = projected[:, inner:]
    live_row = live[0]
    query_live = live_row.astype(jnp.float32)
    live_mark = live_row.astype(jnp.bfloat16)
    upstream = cotangent[0]
    grad_att = (against(upstream, full_out) * query_live[:, None]).astype(jnp.bfloat16)
    neighbours = -(-WIN // length)
    offsets = list(range(neighbours, 0, -1)) + list(range(-1, -neighbours - 1, -1))
    before_pairs, before_marks, after_pairs, after_marks = ([], [], [], [])
    for offset in offsets:
        distance = abs(offset)
        row_count = min(length, WIN - (distance - 1) * length)
        if offset > 0:
            send_pairs = key_values
            send_marks = live_mark
        else:
            send_pairs = key_values
            send_marks = live_mark
        got_pairs, got_marks = from_behind((send_pairs, send_marks), "seq", offset)
        if offset > 0:
            before_pairs.append(got_pairs)
            before_marks.append(got_marks)
        else:
            after_pairs.append(got_pairs)
            after_marks.append(got_marks)
    ext_pairs = jnp.concatenate(before_pairs + [key_values] + after_pairs, axis=0)
    ext_live = jnp.concatenate(before_marks + [live_mark] + after_marks, axis=0).astype(jnp.float32)
    total_span = length + 2 * WIN
    block_rows = min(length, 512)
    key_span = block_rows + 2 * WIN
    query_pos = jnp.arange(block_rows, dtype=jnp.int32)
    key_pos = jnp.arange(key_span, dtype=jnp.int32) - WIN
    in_window = jnp.abs(query_pos[:, None] - key_pos[None, :]) <= WIN
    allowances = [in_window & (ext_live[None, :] > 0.5)]
    score_scale = 1.0 / math.sqrt(HEAD_DIM)

    def split_heads(matrix):
        return matrix.reshape(matrix.shape[0], heads, HEAD_DIM).transpose(1, 0, 2)

    def merge_heads(matrix):
        return matrix.transpose(1, 0, 2).reshape(matrix.shape[1], inner)

    def one_head(inputs):
        query_head, key_head, value_head, grad_head = inputs
        out_blocks, query_blocks = ([], [])
        key_grads = jnp.zeros((total_span, HEAD_DIM), jnp.float32)
        value_grads = jnp.zeros((total_span, HEAD_DIM), jnp.float32)
        attended, grad_query, grad_key, grad_value = head_terms(
            query_head, key_head, value_head, grad_head, allowances[0], query_live, score_scale
        )
        out_blocks.append(attended)
        query_blocks.append(grad_query)
        key_grads = key_grads.at[0:key_span].add(grad_key)
        value_grads = value_grads.at[0:key_span].add(grad_value)
        return (
            jnp.concatenate(out_blocks, axis=0),
            jnp.concatenate(query_blocks, axis=0),
            key_grads,
            value_grads,
        )

    att_heads, query_heads, key_heads, value_heads = lax.map(
        one_head,
        (
            split_heads(query),
            split_heads(ext_pairs[:, :inner]),
            split_heads(ext_pairs[:, inner:]),
            split_heads(grad_att),
        ),
    )
    attention = merge_heads(att_heads)
    grad_query = merge_heads(query_heads)
    ext_grads = jnp.concatenate([merge_heads(key_heads), merge_heads(value_heads)], axis=1)
    own_grads = ext_grads[WIN : WIN + length]
    for offset in offsets:
        distance = abs(offset)
        row_count = min(length, WIN - (distance - 1) * length)
        if offset > 0:
            first_row = WIN - distance * length + length - row_count
        else:
            first_row = WIN + length + (distance - 1) * length
        arrived = from_behind(ext_grads[first_row : first_row + row_count], "seq", -offset)
        if offset > 0:
            own_grads = own_grads.at[length - row_count :].add(arrived)
        else:
            own_grads = own_grads.at[:row_count].add(arrived)
    grad_projected = jnp.concatenate([grad_query, own_grads], axis=1).astype(jnp.bfloat16)
    grad_unit = against(grad_projected, full_qkv) * norm_gain
    through = inverse * (
        grad_unit
        - jnp.mean(grad_unit, axis=-1, keepdims=True)
        - unit_rows * jnp.mean(grad_unit * unit_rows, axis=-1, keepdims=True)
    )
    grad_rows = (upstream.astype(jnp.float32) + through).astype(jnp.bfloat16)[None]
    factor = 1.0 / math.sqrt(n_data * n_seq * length)

    def blocked(left, right):
        left_tiles = left.reshape(length, n_data, left.shape[1] // n_data)
        right_tiles = right.reshape(length, n_seq, right.shape[1] // n_seq)
        tile_grid = jnp.einsum(
            "fpr,fsc->psrc", left_tiles, right_tiles, preferred_element_type=jnp.float32
        )
        return tile_grid.reshape(n_data * n_seq * left_tiles.shape[2], right_tiles.shape[2])

    sum_qkv, sum_out = (
        lax.psum_scatter(
            blocked(normed, grad_projected), ("dp", "seq"), scatter_dimension=0, tiled=True
        ),
        lax.psum_scatter(
            blocked(attention, upstream), ("dp", "seq"), scatter_dimension=0, tiled=True
        ),
    )
    return (grad_rows, sum_qkv * factor, sum_out * factor)


def swap(value, flip):
    count = lax.axis_size("seq")
    return lax.ppermute(value, "seq", [(source, source ^ flip) for source in range(count)])


def attend_kernel(score_scale, blocks, q_ref, g_ref, k_ref, v_ref, ends_ref, live_ref, qlive_ref,
                  att_ref, dq_ref, own_ref, other_ref, bias_ref):
    rows = q_ref.shape[1] // blocks
    span = k_ref.shape[1]

    @pl.when(pl.program_id(0) == 0)
    def _():
        for block in range(blocks):
            columns = slice(block * rows, (block + 1) * rows)
            near = jnp.abs(ends_ref[...] - qlive_ref[0:1, columns]) <= WIN
            bias_ref[:, columns] = jnp.where(near & (live_ref[...] > 0.5), 0.0, NEG)

    key_t, value_t = k_ref[...], v_ref[...]
    key = key_t.T
    value = value_t.T
    key_grad = jnp.zeros((span, HEAD_DIM), jnp.float32)
    value_grad = jnp.zeros((span, HEAD_DIM), jnp.float32)
    for block in range(blocks):
        columns = slice(block * rows, (block + 1) * rows)
        query_t, grad_t = q_ref[:, columns], g_ref[:, columns]
        scores = jnp.dot(key, query_t, preferred_element_type=jnp.float32) * score_scale
        scores = scores + bias_ref[:, columns]
        exponent = jnp.exp(scores - jnp.max(scores, axis=0, keepdims=True))
        inverse = 1.0 / jnp.sum(exponent, axis=0, keepdims=True)
        probabilities = exponent * inverse
        probs_b = probabilities.astype(jnp.bfloat16)
        mixed = jnp.dot(value_t, probs_b, preferred_element_type=jnp.float32)
        attended = (mixed * qlive_ref[1:2, columns]).astype(jnp.bfloat16)
        att_ref[:, columns] = attended
        row_delta = jnp.sum(
            grad_t.astype(jnp.float32) * attended.astype(jnp.float32), axis=0, keepdims=True
        )
        grad_probs = jnp.dot(value, grad_t, preferred_element_type=jnp.float32)
        grad_scores = (probabilities * ((grad_probs - row_delta) * score_scale)).astype(
            jnp.bfloat16
        )
        dq_ref[:, columns] = jnp.dot(
            key_t, grad_scores, preferred_element_type=jnp.float32
        ).astype(jnp.bfloat16)
        key_grad += against(grad_scores, query_t)
        value_grad += against(probs_b, grad_t)
    half = span // 2
    key_grad_t, value_grad_t = key_grad.T, value_grad.T
    own_ref[0] = key_grad_t[:, :half]
    own_ref[1] = value_grad_t[:, :half]
    other_ref[0] = key_grad_t[:, half:].astype(jnp.bfloat16)
    other_ref[1] = value_grad_t[:, half:].astype(jnp.bfloat16)


def attend(query_t, grad_t, key_t, value_t, key_pos, key_live, query_rows, blocks, score_scale):
    features, queries = query_t.shape
    span = key_t.shape[1]
    half = span // 2
    heads = features // HEAD_DIM
    by_query = pl.BlockSpec((HEAD_DIM, queries), lambda h: (h, 0))
    by_key = pl.BlockSpec((HEAD_DIM, span), lambda h: (h, 0))
    grads = pl.BlockSpec((2, HEAD_DIM, half), lambda h: (0, h, 0))
    return pl.pallas_call(
        functools.partial(attend_kernel, score_scale, blocks),
        grid=(heads,),
        in_specs=[
            by_query,
            by_query,
            by_key,
            by_key,
            pl.BlockSpec((span, 1), lambda h: (0, 0)),
            pl.BlockSpec((span, 1), lambda h: (0, 0)),
            pl.BlockSpec((2, queries), lambda h: (0, 0)),
        ],
        out_specs=[by_query, by_query, grads, grads],
        out_shape=[
            jax.ShapeDtypeStruct((features, queries), jnp.bfloat16),
            jax.ShapeDtypeStruct((features, queries), jnp.bfloat16),
            jax.ShapeDtypeStruct((2, features, half), jnp.float32),
            jax.ShapeDtypeStruct((2, features, half), jnp.bfloat16),
        ],
        scratch_shapes=[pltpu.VMEM((span, queries), jnp.float32)],
        compiler_params=pltpu.CompilerParams(vmem_limit_bytes=40 * 2**20),
        cost_estimate=pl.CostEstimate(
            flops=10 * features * queries * span,
            bytes_accessed=12 * features * span,
            transcendentals=heads * queries * span,
        ),
    )(query_t, grad_t, key_t, value_t, key_pos, key_live, query_rows)


def head_body(frames, live, norm_gain, w_qkv, w_out, cotangent):
    length, width = frames.shape[1:]
    n_data = lax.axis_size("dp")
    n_seq = lax.axis_size("seq")
    me = lax.axis_index("seq")
    high, low = me // 2, me % 2
    shard = w_qkv.shape[0]
    inner = w_qkv.shape[1] // 3
    part = inner // 2
    score_scale = 1.0 / math.sqrt(HEAD_DIM)

    mine_qkv = lax.dynamic_index_in_dim(w_qkv.reshape(shard, 3, 2, part), high, 2, keepdims=False)
    mine_qkv = lax.dynamic_slice_in_dim(
        mine_qkv.reshape(shard, 3 * part), low * (shard // 2), shard // 2, 0
    )
    mine_out = lax.dynamic_slice_in_dim(w_out, low * (width // 2), width // 2, 1)
    gathered = lax.all_gather(
        jnp.concatenate([mine_qkv, mine_out], axis=1), "dp", axis=0, tiled=True
    )

    upstream = cotangent[0]
    marks = jnp.zeros((16, width), jnp.bfloat16).at[0, :length].set(live[0].astype(jnp.bfloat16))
    packed = jnp.concatenate([frames[0], marks], axis=0)
    packs = [packed, swap(packed, 2), swap(packed, 1), swap(packed, 3)]
    cots = jnp.concatenate([upstream, swap(upstream, 2)], axis=0)
    rows = jnp.concatenate([pack[:length] for pack in packs], axis=0)
    key_live = jnp.concatenate([pack[length, :length] for pack in packs], axis=0)
    key_live = key_live.astype(jnp.float32)
    step = jnp.arange(length, dtype=jnp.float32)
    key_pos = jnp.concatenate(
        [step + ((me ^ flip) * length).astype(jnp.float32) for flip in (0, 2, 1, 3)]
    )
    queries = 2 * length
    query_live = key_live[:queries]

    unit_rows, inverse = norm_rows(rows.astype(jnp.float32))
    normed = (unit_rows * norm_gain).astype(jnp.bfloat16)

    other_qkv = swap(gathered[:, : 3 * part], 1)
    own_out = lax.dynamic_slice_in_dim(gathered[:, 3 * part :], high * part, part, 0)
    other_out = swap(own_out, 1)
    own_qkv = gathered[:, : 3 * part]
    first = low == 0

    def ordered(own, other, axis):
        return jnp.concatenate(
            [jnp.where(first, own, other), jnp.where(first, other, own)], axis=axis
        )

    part_qkv = ordered(
        own_qkv.reshape(n_data, shard // 2, 3 * part),
        other_qkv.reshape(n_data, shard // 2, 3 * part),
        1,
    ).reshape(n_data * shard, 3 * part)
    part_out = ordered(own_out, other_out, 1)

    def turned(weights, values):
        return lax.dot_general(
            weights, values, (((0,), (1,)), ((), ())), preferred_element_type=jnp.float32
        )

    query_t = turned(part_qkv[:, :part], normed[:queries]).astype(jnp.bfloat16)
    pairs_t = turned(part_qkv[:, part:], normed).astype(jnp.bfloat16)
    grad_t = (against(part_out, cots) * query_live[None, :]).astype(jnp.bfloat16)

    query_rows = jnp.stack([key_pos[:queries], query_live])
    att_t, dq_t, own_grads, other_grads = attend(
        query_t, grad_t, pairs_t[:part], pairs_t[part:],
        key_pos[:, None], key_live[:, None], query_rows, 2, score_scale,
    )
    own_grads = own_grads + swap(other_grads, 1).astype(jnp.float32)

    block = width // n_seq
    partial_out = jnp.dot(att_t, cots, preferred_element_type=jnp.float32)

    def columns_of(flip):
        return lax.dynamic_slice_in_dim(partial_out, (me ^ flip) * block, block, 1)

    arrived = [swap(columns_of(flip).astype(jnp.bfloat16), flip) for flip in (1, 2, 3)]
    arrived = [value.astype(jnp.float32) for value in arrived]
    same, across = columns_of(0) + arrived[0], arrived[1] + arrived[2]
    sum_out = jnp.concatenate(
        [jnp.where(high == 0, same, across), jnp.where(high == 0, across, same)], axis=0
    )

    grads_t = jnp.concatenate(
        [dq_t, own_grads.reshape(2 * part, queries).astype(jnp.bfloat16)], axis=0
    )
    unit = part // 2
    units = grads_t.reshape(6, unit, queries)
    kept = jnp.array([[0, 1, 4], [2, 3, 5], [2, 3, 0], [4, 5, 1]], jnp.int32)

    def pick(index):
        chosen = lax.dynamic_index_in_dim(kept, index, 0, keepdims=False)
        return jnp.concatenate(
            [lax.dynamic_slice_in_dim(units, chosen[i], 1, 0)[0] for i in range(3)], axis=0
        )

    keep_t = jnp.concatenate([pick(me), swap(pick(me ^ 1), 1)], axis=1)
    sum_qkv = lax.dot_general(
        normed, keep_t, (((0,), (1,)), ((), ())), preferred_element_type=jnp.float32
    )

    def through_weights(piece):
        return lax.dot_general(
            piece, part_qkv, (((0,), (1,)), ((), ())), preferred_element_type=jnp.float32
        )

    sent = through_weights(grads_t[:, length:]).astype(jnp.bfloat16)
    grad_unit = through_weights(grads_t[:, :length]) + swap(sent, 2).astype(jnp.float32)
    grad_unit = grad_unit * norm_gain
    own_unit = unit_rows[:length]
    through = inverse[:length] * (
        grad_unit
        - jnp.mean(grad_unit, axis=-1, keepdims=True)
        - own_unit * jnp.mean(grad_unit * own_unit, axis=-1, keepdims=True)
    )
    grad_rows = (upstream.astype(jnp.float32) + through).astype(jnp.bfloat16)[None]

    out_rows = sum_out.shape[0] // n_data
    stacked = jnp.concatenate(
        [sum_qkv, sum_out.reshape(n_data * shard, out_rows * block // shard)], axis=1
    ).astype(jnp.bfloat16)
    total = lax.psum_scatter(stacked, "dp", scatter_dimension=0, tiled=True)
    factor = 1.0 / math.sqrt(n_data * n_seq * length)
    moved = swap(total[:, 2 * unit : 3 * unit], 2)
    own = total[:, : 2 * unit]
    tile_qkv = jnp.where(
        first,
        jnp.concatenate([own, moved], axis=1),
        jnp.concatenate([moved, own], axis=1),
    ).astype(jnp.float32)
    tile_out = total[:, 3 * unit :].astype(jnp.float32).reshape(out_rows, block)
    return (grad_rows, tile_qkv * factor, tile_out * factor)


def solution(mesh):
    n_seq = mesh.shape["seq"]

    def whole(frames, live, norm_gain, w_qkv, w_out, cotangent):
        heads_fit = n_seq == 4 and frames.shape[1] <= frames.shape[1] // n_seq + 2 * WIN
        chosen = head_body if heads_fit else body
        return split(chosen, mesh)(frames, live, norm_gain, w_qkv, w_out, cotangent)

    return whole


def split(chosen, mesh):
    return jax.shard_map(
        chosen,
        mesh=mesh,
        in_specs=(
            P("dp", "seq", None),
            P("dp", "seq"),
            P(),
            P("dp", None),
            P("dp", None),
            P("dp", "seq", None),
        ),
        out_specs=(P("dp", "seq", None), P("dp", "seq"), P("dp", "seq")),
        check_vma=False,
    )
```

```python
import functools
import math

import jax
import jax.numpy as jnp
from jax import lax
from jax.experimental import pallas as pl
from jax.experimental.pallas import tpu as pltpu
from jax.sharding import PartitionSpec as P

HEAD_DIM = 64
WIN = 512


EPS = 1e-05
NEG = -1e30


def from_behind(value, axis, steps):
    count = lax.axis_size(axis)
    leading, last = (max(0, -steps), min(count, count - steps))
    return lax.ppermute(value, axis, [(source, source + steps) for source in range(leading, last)])


def norm_rows(values_in):
    average = jnp.mean(values_in, axis=-1, keepdims=True)
    centred = values_in - average
    inverse = lax.rsqrt(jnp.mean(centred * centred, axis=-1, keepdims=True) + EPS)
    return (centred * inverse, inverse)


def against(left, right):
    return lax.dot_general(
        left, right, (((1,), (1,)), ((), ())), preferred_element_type=jnp.float32
    )


def leading(left, right):
    return lax.dot_general(
        left, right, (((0,), (0,)), ((), ())), preferred_element_type=jnp.float32
    )


def head_terms(query_head, key_head, value_head, grad_head, allowed, query_live, score_scale):
    scores = jnp.where(allowed, against(query_head, key_head) * score_scale, NEG)
    row_peak = jnp.max(scores, axis=-1, keepdims=True)
    exponent = jnp.exp(scores - row_peak)
    probabilities = exponent / jnp.sum(exponent, axis=-1, keepdims=True)
    probs_b = probabilities.astype(jnp.bfloat16)
    mixed = jnp.dot(probs_b, value_head, preferred_element_type=jnp.float32) * query_live[:, None]
    attended = mixed.astype(jnp.bfloat16)
    row_delta = jnp.sum(grad_head.astype(jnp.float32) * attended.astype(jnp.float32), axis=1)
    grad_probs = against(grad_head, value_head)
    grad_scores = (probabilities * (grad_probs - row_delta[:, None]) * score_scale).astype(
        jnp.bfloat16
    )
    grad_query = jnp.dot(grad_scores, key_head, preferred_element_type=jnp.float32)
    grad_key = leading(grad_scores, query_head)
    grad_value = leading(probs_b, grad_head)
    return (attended, grad_query, grad_key, grad_value)


def body(frames, live, norm_gain, w_qkv, w_out, cotangent):
    length = frames.shape[1]
    n_data = lax.axis_size("dp")
    n_seq = lax.axis_size("seq")
    full_qkv, full_out = (
        lax.all_gather(w_qkv, "dp", axis=0, tiled=True),
        lax.all_gather(w_out, "dp", axis=0, tiled=True),
    )
    inner = full_out.shape[0]
    heads = inner // HEAD_DIM
    hidden = frames[0].astype(jnp.float32)
    unit_rows, inverse = norm_rows(hidden)
    normed = (unit_rows * norm_gain).astype(jnp.bfloat16)
    projected = jnp.dot(normed, full_qkv, preferred_element_type=jnp.float32).astype(jnp.bfloat16)
    query = projected[:, :inner]
    key_values = projected[:, inner:]
    live_row = live[0]
    query_live = live_row.astype(jnp.float32)
    live_mark = live_row.astype(jnp.bfloat16)
    upstream = cotangent[0]
    grad_att = (against(upstream, full_out) * query_live[:, None]).astype(jnp.bfloat16)
    neighbours = -(-WIN // length)
    offsets = list(range(neighbours, 0, -1)) + list(range(-1, -neighbours - 1, -1))
    before_pairs, before_marks, after_pairs, after_marks = ([], [], [], [])
    for offset in offsets:
        distance = abs(offset)
        row_count = min(length, WIN - (distance - 1) * length)
        if offset > 0:
            send_pairs = key_values
            send_marks = live_mark
        else:
            send_pairs = key_values
            send_marks = live_mark
        got_pairs, got_marks = from_behind((send_pairs, send_marks), "seq", offset)
        if offset > 0:
            before_pairs.append(got_pairs)
            before_marks.append(got_marks)
        else:
            after_pairs.append(got_pairs)
            after_marks.append(got_marks)
    ext_pairs = jnp.concatenate(before_pairs + [key_values] + after_pairs, axis=0)
    ext_live = jnp.concatenate(before_marks + [live_mark] + after_marks, axis=0).astype(jnp.float32)
    total_span = length + 2 * WIN
    block_rows = min(length, 512)
    key_span = block_rows + 2 * WIN
    query_pos = jnp.arange(block_rows, dtype=jnp.int32)
    key_pos = jnp.arange(key_span, dtype=jnp.int32) - WIN
    in_window = jnp.abs(query_pos[:, None] - key_pos[None, :]) <= WIN
    allowances = [in_window & (ext_live[None, :] > 0.5)]
    score_scale = 1.0 / math.sqrt(HEAD_DIM)

    def split_heads(matrix):
        return matrix.reshape(matrix.shape[0], heads, HEAD_DIM).transpose(1, 0, 2)

    def merge_heads(matrix):
        return matrix.transpose(1, 0, 2).reshape(matrix.shape[1], inner)

    def one_head(inputs):
        query_head, key_head, value_head, grad_head = inputs
        out_blocks, query_blocks = ([], [])
        key_grads = jnp.zeros((total_span, HEAD_DIM), jnp.float32)
        value_grads = jnp.zeros((total_span, HEAD_DIM), jnp.float32)
        attended, grad_query, grad_key, grad_value = head_terms(
            query_head, key_head, value_head, grad_head, allowances[0], query_live, score_scale
        )
        out_blocks.append(attended)
        query_blocks.append(grad_query)
        key_grads = key_grads.at[0:key_span].add(grad_key)
        value_grads = value_grads.at[0:key_span].add(grad_value)
        return (
            jnp.concatenate(out_blocks, axis=0),
            jnp.concatenate(query_blocks, axis=0),
            key_grads,
            value_grads,
        )

    att_heads, query_heads, key_heads, value_heads = lax.map(
        one_head,
        (
            split_heads(query),
            split_heads(ext_pairs[:, :inner]),
            split_heads(ext_pairs[:, inner:]),
            split_heads(grad_att),
        ),
    )
    attention = merge_heads(att_heads)
    grad_query = merge_heads(query_heads)
    ext_grads = jnp.concatenate([merge_heads(key_heads), merge_heads(value_heads)], axis=1)
    own_grads = ext_grads[WIN : WIN + length]
    for offset in offsets:
        distance = abs(offset)
        row_count = min(length, WIN - (distance - 1) * length)
        if offset > 0:
            first_row = WIN - distance * length + length - row_count
        else:
            first_row = WIN + length + (distance - 1) * length
        arrived = from_behind(ext_grads[first_row : first_row + row_count], "seq", -offset)
        if offset > 0:
            own_grads = own_grads.at[length - row_count :].add(arrived)
        else:
            own_grads = own_grads.at[:row_count].add(arrived)
    grad_projected = jnp.concatenate([grad_query, own_grads], axis=1).astype(jnp.bfloat16)
    grad_unit = against(grad_projected, full_qkv) * norm_gain
    through = inverse * (
        grad_unit
        - jnp.mean(grad_unit, axis=-1, keepdims=True)
        - unit_rows * jnp.mean(grad_unit * unit_rows, axis=-1, keepdims=True)
    )
    grad_rows = (upstream.astype(jnp.float32) + through).astype(jnp.bfloat16)[None]
    factor = 1.0 / math.sqrt(n_data * n_seq * length)

    def blocked(left, right):
        left_tiles = left.reshape(length, n_data, left.shape[1] // n_data)
        right_tiles = right.reshape(length, n_seq, right.shape[1] // n_seq)
        tile_grid = jnp.einsum(
            "fpr,fsc->psrc", left_tiles, right_tiles, preferred_element_type=jnp.float32
        )
        return tile_grid.reshape(n_data * n_seq * left_tiles.shape[2], right_tiles.shape[2])

    sum_qkv, sum_out = (
        lax.psum_scatter(
            blocked(normed, grad_projected), ("dp", "seq"), scatter_dimension=0, tiled=True
        ),
        lax.psum_scatter(
            blocked(attention, upstream), ("dp", "seq"), scatter_dimension=0, tiled=True
        ),
    )
    return (grad_rows, sum_qkv * factor, sum_out * factor)


def swap(value, flip):
    count = lax.axis_size("seq")
    return lax.ppermute(value, "seq", [(source, source ^ flip) for source in range(count)])


def attend_kernel(score_scale, blocks, q_ref, g_ref, k_ref, v_ref, ends_ref, live_ref, qlive_ref,
                  att_ref, dq_ref, own_ref, other_ref, bias_ref):
    rows = q_ref.shape[1] // blocks
    span = k_ref.shape[1]

    @pl.when(pl.program_id(0) == 0)
    def _():
        for block in range(blocks):
            columns = slice(block * rows, (block + 1) * rows)
            near = jnp.abs(ends_ref[...] - qlive_ref[0:1, columns]) <= WIN
            bias_ref[:, columns] = jnp.where(near & (live_ref[...] > 0.5), 0.0, NEG)

    key_t, value_t = k_ref[...], v_ref[...]
    key = key_t.T
    value = value_t.T
    key_grad = jnp.zeros((span, HEAD_DIM), jnp.float32)
    value_grad = jnp.zeros((span, HEAD_DIM), jnp.float32)
    for block in range(blocks):
        columns = slice(block * rows, (block + 1) * rows)
        query_t, grad_t = q_ref[:, columns], g_ref[:, columns]
        scores = jnp.dot(key, query_t, preferred_element_type=jnp.float32) * score_scale
        scores = scores + bias_ref[:, columns]
        exponent = jnp.exp(scores - jnp.max(scores, axis=0, keepdims=True))
        inverse = 1.0 / jnp.sum(exponent, axis=0, keepdims=True)
        probabilities = exponent * inverse
        probs_b = probabilities.astype(jnp.bfloat16)
        mixed = jnp.dot(value_t, probs_b, preferred_element_type=jnp.float32)
        attended = (mixed * qlive_ref[1:2, columns]).astype(jnp.bfloat16)
        att_ref[:, columns] = attended
        row_delta = jnp.sum(
            grad_t.astype(jnp.float32) * attended.astype(jnp.float32), axis=0, keepdims=True
        )
        grad_probs = jnp.dot(value, grad_t, preferred_element_type=jnp.float32)
        grad_scores = (probabilities * ((grad_probs - row_delta) * score_scale)).astype(
            jnp.bfloat16
        )
        dq_ref[:, columns] = jnp.dot(
            key_t, grad_scores, preferred_element_type=jnp.float32
        ).astype(jnp.bfloat16)
        key_grad += against(grad_scores, query_t)
        value_grad += against(probs_b, grad_t)
    half = span // 2
    key_grad_t, value_grad_t = key_grad.T, value_grad.T
    own_ref[0] = key_grad_t[:, :half]
    own_ref[1] = value_grad_t[:, :half]
    other_ref[0] = key_grad_t[:, half:].astype(jnp.bfloat16)
    other_ref[1] = value_grad_t[:, half:].astype(jnp.bfloat16)


def attend(query_t, grad_t, key_t, value_t, key_pos, key_live, query_rows, blocks, score_scale):
    features, queries = query_t.shape
    span = key_t.shape[1]
    half = span // 2
    heads = features // HEAD_DIM
    by_query = pl.BlockSpec((HEAD_DIM, queries), lambda h: (h, 0))
    by_key = pl.BlockSpec((HEAD_DIM, span), lambda h: (h, 0))
    grads = pl.BlockSpec((2, HEAD_DIM, half), lambda h: (0, h, 0))
    return pl.pallas_call(
        functools.partial(attend_kernel, score_scale, blocks),
        grid=(heads,),
        in_specs=[
            by_query,
            by_query,
            by_key,
            by_key,
            pl.BlockSpec((span, 1), lambda h: (0, 0)),
            pl.BlockSpec((span, 1), lambda h: (0, 0)),
            pl.BlockSpec((2, queries), lambda h: (0, 0)),
        ],
        out_specs=[by_query, by_query, grads, grads],
        out_shape=[
            jax.ShapeDtypeStruct((features, queries), jnp.bfloat16),
            jax.ShapeDtypeStruct((features, queries), jnp.bfloat16),
            jax.ShapeDtypeStruct((2, features, half), jnp.float32),
            jax.ShapeDtypeStruct((2, features, half), jnp.bfloat16),
        ],
        scratch_shapes=[pltpu.VMEM((span, queries), jnp.float32)],
        compiler_params=pltpu.CompilerParams(vmem_limit_bytes=40 * 2**20),
        cost_estimate=pl.CostEstimate(
            flops=10 * features * queries * span,
            bytes_accessed=12 * features * span,
            transcendentals=heads * queries * span,
        ),
    )(query_t, grad_t, key_t, value_t, key_pos, key_live, query_rows)


MESH = pl.DeviceIdType.MESH


def gather_kernel(piece_ref, out_ref, line_send, line_recv, side_send, side_recv,
                  core_send, core_recv, local_sem):
    count = out_ref.shape[0]
    dp, seq = lax.axis_index("dp"), lax.axis_index("seq")
    z, x, core = dp // 2, dp % 2, seq % 2
    mate = seq + 1 - 2 * core
    steps = 2 * count - 1
    above, below = z < count - 1, z > 0

    barrier = pltpu.get_barrier_semaphore()
    pl.semaphore_signal(barrier, inc=1, device_id={"dp": 2 * z + 1 - x}, device_id_type=MESH)
    pl.semaphore_signal(barrier, inc=1, device_id={"seq": mate}, device_id_type=MESH)

    @pl.when(above)
    def _():
        pl.semaphore_signal(barrier, inc=1, device_id={"dp": dp + 2}, device_id_type=MESH)

    @pl.when(below)
    def _():
        pl.semaphore_signal(barrier, inc=1, device_id={"dp": dp - 2}, device_id_type=MESH)

    pl.semaphore_wait(barrier, 2 + above.astype(jnp.int32) + below.astype(jnp.int32))

    def line(hop, up):
        origin = z - hop if up else z + hop
        source = piece_ref if hop == 0 else out_ref.at[origin, x, core]
        flow = 0 if up else 1
        return pltpu.make_async_remote_copy(
            src_ref=source, dst_ref=out_ref.at[origin, x, core],
            send_sem=line_send.at[flow, hop], recv_sem=line_recv.at[flow, hop],
            device_id={"dp": dp + 2 if up else dp - 2}, device_id_type=MESH,
        )

    def line_arrival(hop, up):
        origin = z - hop if up else z + hop
        flow = 0 if up else 1
        return pltpu.make_async_remote_copy(
            src_ref=piece_ref, dst_ref=out_ref.at[origin, x, core],
            send_sem=line_send.at[flow, hop - 1], recv_sem=line_recv.at[flow, hop - 1],
            device_id={"dp": dp + 2 if up else dp - 2}, device_id_type=MESH,
        )

    def side(step, origin, column):
        source = piece_ref if step == 0 else out_ref.at[origin, x, core]
        return pltpu.make_async_remote_copy(
            src_ref=source, dst_ref=out_ref.at[origin, column, core],
            send_sem=side_send.at[step], recv_sem=side_recv.at[step],
            device_id={"dp": 2 * z + 1 - x}, device_id_type=MESH,
        )

    def across(slot, origin, column, half):
        source = piece_ref if slot == 0 else out_ref.at[origin, column, core]
        return pltpu.make_async_remote_copy(
            src_ref=source, dst_ref=out_ref.at[origin, column, half],
            send_sem=core_send.at[slot], recv_sem=core_recv.at[slot],
            device_id={"seq": mate}, device_id_type=MESH,
        )

    waves = [(0, z, None)]
    for hop in range(1, count):
        waves.append((hop, z - hop, z >= hop))
        waves.append((count - 1 + hop, z + hop, z + hop < count))

    def guarded(condition, action):
        if condition is None:
            action()
        else:
            pl.when(condition)(action)

    keep = pltpu.make_async_copy(piece_ref, out_ref.at[z, x, core], local_sem)
    keep.start()
    pl.when(above)(lambda: line(0, True).start())
    pl.when(below)(lambda: line(0, False).start())
    side(0, z, x).start()
    across(0, z, x, core).start()

    def side_wave(step, origin):
        side(step, origin, 1 - x).wait_recv()
        across(steps + step, origin, 1 - x, core).start()

    for step, origin, condition in waves[1:]:
        up = step < count
        hop = step if up else step - count + 1

        def forward(step=step, origin=origin, up=up, hop=hop):
            line_arrival(hop, up).wait_recv()
            if hop < count - 1:
                pl.when(above if up else below)(lambda: line(hop, up).start())
            side(step, origin, x).start()
            across(step, origin, x, core).start()

        guarded(condition, forward)
        if not up:
            for late, place, holds in waves:
                late_hop = late if late < count else late - count + 1
                if late_hop == hop - 1:
                    guarded(holds, functools.partial(side_wave, late, place))
    for late, place, holds in waves[-2:]:
        guarded(holds, functools.partial(side_wave, late, place))

    keep.wait()
    for step, origin, condition in waves:
        def finish(step=step, origin=origin):
            side(step, origin, x).wait_send()
            across(step, origin, x, core).wait_send()
            across(steps + step, origin, 1 - x, core).wait_send()
            across(step, origin, x, 1 - core).wait_recv()
            across(steps + step, origin, 1 - x, 1 - core).wait_recv()
            up = step < count
            hop = step if up else step - count + 1
            if step == 0:
                pl.when(above)(lambda: line(0, True).wait_send())
                pl.when(below)(lambda: line(0, False).wait_send())
            elif hop < count - 1:
                pl.when(above if up else below)(lambda: line(hop, up).wait_send())

        guarded(condition, finish)


def gather_pieces(piece, count):
    steps = 2 * count - 1
    dma = pltpu.SemaphoreType.DMA
    return pl.pallas_call(
        gather_kernel,
        out_shape=jax.ShapeDtypeStruct((count, 2, 2) + piece.shape, piece.dtype),
        in_specs=[pl.BlockSpec(memory_space=pltpu.VMEM)],
        out_specs=pl.BlockSpec(memory_space=pltpu.VMEM),
        scratch_shapes=[
            dma((2, count)), dma((2, count)), dma((steps,)), dma((steps,)),
            dma((2 * steps,)), dma((2 * steps,)), dma(()),
        ],
        compiler_params=pltpu.CompilerParams(
            collective_id=0, has_side_effects=True, vmem_limit_bytes=24 * 2**20
        ),
        cost_estimate=pl.CostEstimate(
            flops=0, bytes_accessed=64 * piece.size * count, transcendentals=0
        ),
    )(piece)


def sum_kernel(chunks, factor, *refs):
    ins, outs = refs[:2], refs[2:4]
    beside, summed, lined = refs[4:6], refs[6:8], refs[8:10]
    side_send, side_recv, line_send, line_recv = refs[10:]
    count = ins[0].shape[0]
    dp = lax.axis_index("dp")
    z, x = dp // 2, dp % 2
    neighbour = 2 * z + 1 - x
    peers = [lax.rem(z + step, count) for step in range(1, count)]

    barrier = pltpu.get_barrier_semaphore()
    pl.semaphore_signal(barrier, inc=1, device_id={"dp": neighbour}, device_id_type=MESH)
    for peer in peers:
        pl.semaphore_signal(barrier, inc=1, device_id={"dp": 2 * peer + x}, device_id_type=MESH)
    pl.semaphore_wait(barrier, count)

    def rows_of(which, chunk):
        size = ins[which].shape[2] // chunks
        return pl.ds(chunk * size, size)

    def side(which, chunk):
        return pltpu.make_async_remote_copy(
            src_ref=ins[which].at[:, 1 - x, rows_of(which, chunk)],
            dst_ref=beside[which].at[chunk],
            send_sem=side_send.at[which, chunk], recv_sem=side_recv.at[which, chunk],
            device_id={"dp": neighbour}, device_id_type=MESH,
        )

    def line(which, chunk, step):
        peer = peers[step]
        return pltpu.make_async_remote_copy(
            src_ref=summed[which].at[chunk, peer],
            dst_ref=lined[which].at[chunk, step],
            send_sem=line_send.at[which, chunk, step], recv_sem=line_recv.at[which, chunk, step],
            device_id={"dp": 2 * peer + x}, device_id_type=MESH,
        )

    both = [(chunk, which) for chunk in range(chunks) for which in (0, 1)]
    for chunk, which in both:
        side(which, chunk).start()
    for chunk, which in both:
        side(which, chunk).wait_recv()
        for step in range(count - 1):
            peer = peers[step]
            summed[which][chunk, peer] = (
                ins[which][peer, x, rows_of(which, chunk)].astype(jnp.float32)
                + beside[which][chunk, peer].astype(jnp.float32)
            ).astype(jnp.bfloat16)
            line(which, chunk, step).start()
    for chunk, which in both:
        total = ins[which][z, x, rows_of(which, chunk)].astype(jnp.float32)
        total = total + beside[which][chunk, z].astype(jnp.float32)
        for step in range(count - 1):
            line(which, chunk, step).wait_recv()
            total = total + lined[which][chunk, step].astype(jnp.float32)
        outs[which][rows_of(which, chunk)] = total * factor
    for chunk, which in both:
        side(which, chunk).wait_send()
        for step in range(count - 1):
            line(which, chunk, step).wait_send()


def sum_tiles(arrays, count, chunks, factor):
    tiles = [a.reshape(count, 2, a.shape[0] // (2 * count), a.shape[1]) for a in arrays]
    vmem = pl.BlockSpec(memory_space=pltpu.VMEM)
    dma = pltpu.SemaphoreType.DMA

    def slots(lead):
        return [
            pltpu.VMEM((chunks, lead, t.shape[2] // chunks, t.shape[3]), t.dtype) for t in tiles
        ]

    return pl.pallas_call(
        functools.partial(sum_kernel, chunks, factor),
        out_shape=[jax.ShapeDtypeStruct(t.shape[2:], jnp.float32) for t in tiles],
        in_specs=[vmem, vmem],
        out_specs=[vmem, vmem],
        scratch_shapes=slots(count) + slots(count) + slots(count - 1) + [
            dma((2, chunks)), dma((2, chunks)),
            dma((2, chunks, count - 1)), dma((2, chunks, count - 1)),
        ],
        compiler_params=pltpu.CompilerParams(
            collective_id=1, has_side_effects=True, vmem_limit_bytes=24 * 2**20
        ),
        cost_estimate=pl.CostEstimate(
            flops=0, bytes_accessed=64 * tiles[0].size, transcendentals=0
        ),
    )(*tiles)


def head_body(frames, live, norm_gain, w_qkv, w_out, cotangent):
    length, width = frames.shape[1:]
    n_data = lax.axis_size("dp")
    n_seq = lax.axis_size("seq")
    me = lax.axis_index("seq")
    high, low = me // 2, me % 2
    shard = w_qkv.shape[0]
    inner = w_qkv.shape[1] // 3
    part = inner // 2
    score_scale = 1.0 / math.sqrt(HEAD_DIM)

    mine_qkv = lax.dynamic_index_in_dim(w_qkv.reshape(shard, 3, 2, part), high, 2, keepdims=False)
    mine_qkv = lax.dynamic_slice_in_dim(
        mine_qkv.reshape(shard, 3 * part), low * (shard // 2), shard // 2, 0
    )
    mine_out = lax.dynamic_slice_in_dim(w_out, low * (width // 2), width // 2, 1)
    packed_weights = jnp.concatenate([mine_out, mine_qkv], axis=1)

    upstream = cotangent[0]
    marks = jnp.zeros((16, width), jnp.bfloat16).at[0, :length].set(live[0].astype(jnp.bfloat16))
    packed = jnp.concatenate([frames[0], marks], axis=0)
    packs = [packed, swap(packed, 2), swap(packed, 1), swap(packed, 3)]
    cots = jnp.concatenate([upstream, swap(upstream, 2)], axis=0)
    rows = jnp.concatenate([pack[:length] for pack in packs], axis=0)
    key_live = jnp.concatenate([pack[length, :length] for pack in packs], axis=0)
    key_live = key_live.astype(jnp.float32)
    step = jnp.arange(length, dtype=jnp.float32)
    key_pos = jnp.concatenate(
        [step + ((me ^ flip) * length).astype(jnp.float32) for flip in (0, 2, 1, 3)]
    )
    queries = 2 * length
    query_live = key_live[:queries]

    unit_rows, inverse = norm_rows(rows.astype(jnp.float32))
    normed = (unit_rows * norm_gain).astype(jnp.bfloat16)

    gathered = gather_pieces(packed_weights, n_data // 2)
    part_qkv = gathered[..., width // 2 :].reshape(n_data * shard, 3 * part)
    halves = gathered[..., : width // 2].reshape(n_data, 2, shard // 2, width // 2)
    halves = lax.dynamic_slice_in_dim(halves, high * (n_data // 2), n_data // 2, 0)
    part_out = jnp.concatenate(
        [halves[:, half].reshape(part, width // 2) for half in (0, 1)], axis=1
    )

    def turned(weights, values):
        return lax.dot_general(
            weights, values, (((0,), (1,)), ((), ())), preferred_element_type=jnp.float32
        )

    query_t = turned(part_qkv[:, :part], normed[:queries]).astype(jnp.bfloat16)
    pairs_t = turned(part_qkv[:, part:], normed).astype(jnp.bfloat16)
    grad_t = (against(part_out, cots) * query_live[None, :]).astype(jnp.bfloat16)

    query_rows = jnp.stack([key_pos[:queries], query_live])
    att_t, dq_t, own_grads, other_grads = attend(
        query_t, grad_t, pairs_t[:part], pairs_t[part:],
        key_pos[:, None], key_live[:, None], query_rows, 2, score_scale,
    )
    own_grads = own_grads + swap(other_grads, 1).astype(jnp.float32)

    block = width // n_seq
    partial_out = jnp.dot(att_t, cots, preferred_element_type=jnp.float32)

    def columns_of(flip):
        return lax.dynamic_slice_in_dim(partial_out, (me ^ flip) * block, block, 1)

    arrived = [swap(columns_of(flip).astype(jnp.bfloat16), flip) for flip in (1, 2, 3)]
    arrived = [value.astype(jnp.float32) for value in arrived]
    same, across = columns_of(0) + arrived[0], arrived[1] + arrived[2]
    sum_out = jnp.concatenate(
        [jnp.where(high == 0, same, across), jnp.where(high == 0, across, same)], axis=0
    )

    grads_t = jnp.concatenate(
        [dq_t, own_grads.reshape(2 * part, queries).astype(jnp.bfloat16)], axis=0
    )
    unit = part // 2

    def units(start, count):
        return lax.dynamic_slice_in_dim(grads_t, start * unit, count * unit, 0)

    beside = swap(units(2 * (high + 1 - low), 2), 1)
    facing = swap(units(4 * (1 - high) + low, 1), 2)
    corner = swap(units(4 * (1 - high) + 1 - low, 1), 3)
    two = jnp.concatenate([units(2 * (high + low), 2), beside], axis=1)
    one = jnp.concatenate(
        [facing[:, length:], facing[:, :length], corner[:, length:], corner[:, :length]], axis=1
    )
    first = low == 0
    keep_t = jnp.where(
        first, jnp.concatenate([two, one], axis=0), jnp.concatenate([one, two], axis=0)
    )
    sum_qkv = lax.dot_general(
        normed, keep_t, (((0,), (1,)), ((), ())), preferred_element_type=jnp.float32
    )

    def through_weights(piece):
        return lax.dot_general(
            piece, part_qkv, (((0,), (1,)), ((), ())), preferred_element_type=jnp.float32
        )

    arrived = swap(through_weights(grads_t[:, length:]).astype(jnp.bfloat16), 2)
    factor = 1.0 / math.sqrt(n_data * n_seq * length)
    tile_qkv, tile_out = sum_tiles(
        [sum_qkv.astype(jnp.bfloat16), sum_out.astype(jnp.bfloat16)], n_data // 2, 5, factor
    )
    grad_unit = through_weights(grads_t[:, :length]) + arrived.astype(jnp.float32)
    grad_unit = grad_unit * norm_gain
    own_unit = unit_rows[:length]
    through = inverse[:length] * (
        grad_unit
        - jnp.mean(grad_unit, axis=-1, keepdims=True)
        - own_unit * jnp.mean(grad_unit * own_unit, axis=-1, keepdims=True)
    )
    grad_rows = (upstream.astype(jnp.float32) + through).astype(jnp.bfloat16)[None]

    return (grad_rows, tile_qkv, tile_out)


def solution(mesh):
    n_seq = mesh.shape["seq"]

    def whole(frames, live, norm_gain, w_qkv, w_out, cotangent):
        heads_fit = n_seq == 4 and mesh.shape["dp"] == 8 and frames.shape[1] <= frames.shape[1] // n_seq + 2 * WIN
        chosen = head_body if heads_fit else body
        return split(chosen, mesh)(frames, live, norm_gain, w_qkv, w_out, cotangent)

    return whole


def split(chosen, mesh):
    return jax.shard_map(
        chosen,
        mesh=mesh,
        in_specs=(
            P("dp", "seq", None),
            P("dp", "seq"),
            P(),
            P("dp", None),
            P("dp", None),
            P("dp", "seq", None),
        ),
        out_specs=(P("dp", "seq", None), P("dp", "seq"), P("dp", "seq")),
        check_vma=False,
    )
```

```python
import functools
import math

import jax
import jax.numpy as jnp
from jax import lax
from jax.experimental import pallas as pl
from jax.experimental.pallas import tpu as pltpu
from jax.sharding import PartitionSpec as P

HEAD_DIM = 64
WIN = 512


EPS = 1e-05
NEG = -1e30


def from_behind(value, axis, steps):
    count = lax.axis_size(axis)
    leading, last = (max(0, -steps), min(count, count - steps))
    return lax.ppermute(value, axis, [(source, source + steps) for source in range(leading, last)])


def norm_rows(values_in):
    average = jnp.mean(values_in, axis=-1, keepdims=True)
    centred = values_in - average
    inverse = lax.rsqrt(jnp.mean(centred * centred, axis=-1, keepdims=True) + EPS)
    return (centred * inverse, inverse)


def against(left, right):
    return lax.dot_general(
        left, right, (((1,), (1,)), ((), ())), preferred_element_type=jnp.float32
    )


def leading(left, right):
    return lax.dot_general(
        left, right, (((0,), (0,)), ((), ())), preferred_element_type=jnp.float32
    )


def head_terms(query_head, key_head, value_head, grad_head, allowed, query_live, score_scale):
    scores = jnp.where(allowed, against(query_head, key_head) * score_scale, NEG)
    row_peak = jnp.max(scores, axis=-1, keepdims=True)
    exponent = jnp.exp(scores - row_peak)
    probabilities = exponent / jnp.sum(exponent, axis=-1, keepdims=True)
    probs_b = probabilities.astype(jnp.bfloat16)
    mixed = jnp.dot(probs_b, value_head, preferred_element_type=jnp.float32) * query_live[:, None]
    attended = mixed.astype(jnp.bfloat16)
    row_delta = jnp.sum(grad_head.astype(jnp.float32) * attended.astype(jnp.float32), axis=1)
    grad_probs = against(grad_head, value_head)
    grad_scores = (probabilities * (grad_probs - row_delta[:, None]) * score_scale).astype(
        jnp.bfloat16
    )
    grad_query = jnp.dot(grad_scores, key_head, preferred_element_type=jnp.float32)
    grad_key = leading(grad_scores, query_head)
    grad_value = leading(probs_b, grad_head)
    return (attended, grad_query, grad_key, grad_value)


def body(frames, live, norm_gain, w_qkv, w_out, cotangent):
    length = frames.shape[1]
    n_data = lax.axis_size("dp")
    n_seq = lax.axis_size("seq")
    full_qkv, full_out = (
        lax.all_gather(w_qkv, "dp", axis=0, tiled=True),
        lax.all_gather(w_out, "dp", axis=0, tiled=True),
    )
    inner = full_out.shape[0]
    heads = inner // HEAD_DIM
    hidden = frames[0].astype(jnp.float32)
    unit_rows, inverse = norm_rows(hidden)
    normed = (unit_rows * norm_gain).astype(jnp.bfloat16)
    projected = jnp.dot(normed, full_qkv, preferred_element_type=jnp.float32).astype(jnp.bfloat16)
    query = projected[:, :inner]
    key_values = projected[:, inner:]
    live_row = live[0]
    query_live = live_row.astype(jnp.float32)
    live_mark = live_row.astype(jnp.bfloat16)
    upstream = cotangent[0]
    grad_att = (against(upstream, full_out) * query_live[:, None]).astype(jnp.bfloat16)
    neighbours = -(-WIN // length)
    offsets = list(range(neighbours, 0, -1)) + list(range(-1, -neighbours - 1, -1))
    before_pairs, before_marks, after_pairs, after_marks = ([], [], [], [])
    for offset in offsets:
        distance = abs(offset)
        row_count = min(length, WIN - (distance - 1) * length)
        if offset > 0:
            send_pairs = key_values
            send_marks = live_mark
        else:
            send_pairs = key_values
            send_marks = live_mark
        got_pairs, got_marks = from_behind((send_pairs, send_marks), "seq", offset)
        if offset > 0:
            before_pairs.append(got_pairs)
            before_marks.append(got_marks)
        else:
            after_pairs.append(got_pairs)
            after_marks.append(got_marks)
    ext_pairs = jnp.concatenate(before_pairs + [key_values] + after_pairs, axis=0)
    ext_live = jnp.concatenate(before_marks + [live_mark] + after_marks, axis=0).astype(jnp.float32)
    total_span = length + 2 * WIN
    block_rows = min(length, 512)
    key_span = block_rows + 2 * WIN
    query_pos = jnp.arange(block_rows, dtype=jnp.int32)
    key_pos = jnp.arange(key_span, dtype=jnp.int32) - WIN
    in_window = jnp.abs(query_pos[:, None] - key_pos[None, :]) <= WIN
    allowances = [in_window & (ext_live[None, :] > 0.5)]
    score_scale = 1.0 / math.sqrt(HEAD_DIM)

    def split_heads(matrix):
        return matrix.reshape(matrix.shape[0], heads, HEAD_DIM).transpose(1, 0, 2)

    def merge_heads(matrix):
        return matrix.transpose(1, 0, 2).reshape(matrix.shape[1], inner)

    def one_head(inputs):
        query_head, key_head, value_head, grad_head = inputs
        out_blocks, query_blocks = ([], [])
        key_grads = jnp.zeros((total_span, HEAD_DIM), jnp.float32)
        value_grads = jnp.zeros((total_span, HEAD_DIM), jnp.float32)
        attended, grad_query, grad_key, grad_value = head_terms(
            query_head, key_head, value_head, grad_head, allowances[0], query_live, score_scale
        )
        out_blocks.append(attended)
        query_blocks.append(grad_query)
        key_grads = key_grads.at[0:key_span].add(grad_key)
        value_grads = value_grads.at[0:key_span].add(grad_value)
        return (
            jnp.concatenate(out_blocks, axis=0),
            jnp.concatenate(query_blocks, axis=0),
            key_grads,
            value_grads,
        )

    att_heads, query_heads, key_heads, value_heads = lax.map(
        one_head,
        (
            split_heads(query),
            split_heads(ext_pairs[:, :inner]),
            split_heads(ext_pairs[:, inner:]),
            split_heads(grad_att),
        ),
    )
    attention = merge_heads(att_heads)
    grad_query = merge_heads(query_heads)
    ext_grads = jnp.concatenate([merge_heads(key_heads), merge_heads(value_heads)], axis=1)
    own_grads = ext_grads[WIN : WIN + length]
    for offset in offsets:
        distance = abs(offset)
        row_count = min(length, WIN - (distance - 1) * length)
        if offset > 0:
            first_row = WIN - distance * length + length - row_count
        else:
            first_row = WIN + length + (distance - 1) * length
        arrived = from_behind(ext_grads[first_row : first_row + row_count], "seq", -offset)
        if offset > 0:
            own_grads = own_grads.at[length - row_count :].add(arrived)
        else:
            own_grads = own_grads.at[:row_count].add(arrived)
    grad_projected = jnp.concatenate([grad_query, own_grads], axis=1).astype(jnp.bfloat16)
    grad_unit = against(grad_projected, full_qkv) * norm_gain
    through = inverse * (
        grad_unit
        - jnp.mean(grad_unit, axis=-1, keepdims=True)
        - unit_rows * jnp.mean(grad_unit * unit_rows, axis=-1, keepdims=True)
    )
    grad_rows = (upstream.astype(jnp.float32) + through).astype(jnp.bfloat16)[None]
    factor = 1.0 / math.sqrt(n_data * n_seq * length)

    def blocked(left, right):
        left_tiles = left.reshape(length, n_data, left.shape[1] // n_data)
        right_tiles = right.reshape(length, n_seq, right.shape[1] // n_seq)
        tile_grid = jnp.einsum(
            "fpr,fsc->psrc", left_tiles, right_tiles, preferred_element_type=jnp.float32
        )
        return tile_grid.reshape(n_data * n_seq * left_tiles.shape[2], right_tiles.shape[2])

    sum_qkv, sum_out = (
        lax.psum_scatter(
            blocked(normed, grad_projected), ("dp", "seq"), scatter_dimension=0, tiled=True
        ),
        lax.psum_scatter(
            blocked(attention, upstream), ("dp", "seq"), scatter_dimension=0, tiled=True
        ),
    )
    return (grad_rows, sum_qkv * factor, sum_out * factor)


def swap(value, flip):
    count = lax.axis_size("seq")
    return lax.ppermute(value, "seq", [(source, source ^ flip) for source in range(count)])


def attend_kernel(score_scale, blocks, q_ref, g_ref, k_ref, v_ref, ends_ref, live_ref, qlive_ref,
                  att_ref, dq_ref, own_ref, other_ref, bias_ref):
    rows = q_ref.shape[1] // blocks
    span = k_ref.shape[1]

    @pl.when(pl.program_id(0) == 0)
    def _():
        for block in range(blocks):
            columns = slice(block * rows, (block + 1) * rows)
            near = jnp.abs(ends_ref[...] - qlive_ref[0:1, columns]) <= WIN
            bias_ref[:, columns] = jnp.where(near & (live_ref[...] > 0.5), 0.0, NEG)

    key_t, value_t = k_ref[...], v_ref[...]
    key = key_t.T
    value = value_t.T
    key_grad = jnp.zeros((span, HEAD_DIM), jnp.float32)
    value_grad = jnp.zeros((span, HEAD_DIM), jnp.float32)
    for block in range(blocks):
        columns = slice(block * rows, (block + 1) * rows)
        query_t, grad_t = q_ref[:, columns], g_ref[:, columns]
        scores = jnp.dot(
            key, (query_t * score_scale).astype(jnp.bfloat16), preferred_element_type=jnp.float32
        )
        scores = scores + bias_ref[:, columns]
        exponent = jnp.exp(scores - jnp.max(scores, axis=0, keepdims=True))
        inverse = 1.0 / jnp.sum(exponent, axis=0, keepdims=True)
        probabilities = exponent * inverse
        probs_b = probabilities.astype(jnp.bfloat16)
        mixed = jnp.dot(value_t, probs_b, preferred_element_type=jnp.float32)
        attended = (mixed * qlive_ref[1:2, columns]).astype(jnp.bfloat16)
        att_ref[:, columns] = attended
        row_delta = jnp.sum(
            grad_t.astype(jnp.float32) * attended.astype(jnp.float32), axis=0, keepdims=True
        )
        grad_probs = jnp.dot(
            value, (grad_t * score_scale).astype(jnp.bfloat16), preferred_element_type=jnp.float32
        )
        grad_scores = (probabilities * (grad_probs - row_delta * score_scale)).astype(
            jnp.bfloat16
        )
        dq_ref[:, columns] = jnp.dot(
            key_t, grad_scores, preferred_element_type=jnp.float32
        ).astype(jnp.bfloat16)
        key_grad += against(grad_scores, query_t)
        value_grad += against(probs_b, grad_t)
    half = span // 2
    key_grad_t, value_grad_t = key_grad.T, value_grad.T
    own_ref[0] = key_grad_t[:, :half]
    own_ref[1] = value_grad_t[:, :half]
    other_ref[0] = key_grad_t[:, half:].astype(jnp.bfloat16)
    other_ref[1] = value_grad_t[:, half:].astype(jnp.bfloat16)


def attend(query_t, grad_t, key_t, value_t, key_pos, key_live, query_rows, blocks, score_scale):
    features, queries = query_t.shape
    span = key_t.shape[1]
    half = span // 2
    heads = features // HEAD_DIM
    by_query = pl.BlockSpec((HEAD_DIM, queries), lambda h: (h, 0))
    by_key = pl.BlockSpec((HEAD_DIM, span), lambda h: (h, 0))
    grads = pl.BlockSpec((2, HEAD_DIM, half), lambda h: (0, h, 0))
    return pl.pallas_call(
        functools.partial(attend_kernel, score_scale, blocks),
        grid=(heads,),
        in_specs=[
            by_query,
            by_query,
            by_key,
            by_key,
            pl.BlockSpec((span, 1), lambda h: (0, 0)),
            pl.BlockSpec((span, 1), lambda h: (0, 0)),
            pl.BlockSpec((2, queries), lambda h: (0, 0)),
        ],
        out_specs=[by_query, by_query, grads, grads],
        out_shape=[
            jax.ShapeDtypeStruct((features, queries), jnp.bfloat16),
            jax.ShapeDtypeStruct((features, queries), jnp.bfloat16),
            jax.ShapeDtypeStruct((2, features, half), jnp.float32),
            jax.ShapeDtypeStruct((2, features, half), jnp.bfloat16),
        ],
        scratch_shapes=[pltpu.VMEM((span, queries), jnp.float32)],
        compiler_params=pltpu.CompilerParams(vmem_limit_bytes=40 * 2**20),
        cost_estimate=pl.CostEstimate(
            flops=10 * features * queries * span,
            bytes_accessed=12 * features * span,
            transcendentals=heads * queries * span,
        ),
    )(query_t, grad_t, key_t, value_t, key_pos, key_live, query_rows)


MESH = pl.DeviceIdType.MESH


def gather_kernel(piece_ref, out_ref, line_send, line_recv, side_send, side_recv,
                  core_send, core_recv, local_sem):
    count = out_ref.shape[0]
    dp, seq = lax.axis_index("dp"), lax.axis_index("seq")
    z, x, core = dp // 2, dp % 2, seq % 2
    mate = seq + 1 - 2 * core
    steps = 2 * count - 1
    above, below = z < count - 1, z > 0

    barrier = pltpu.get_barrier_semaphore()
    pl.semaphore_signal(barrier, inc=1, device_id={"dp": 2 * z + 1 - x}, device_id_type=MESH)
    pl.semaphore_signal(barrier, inc=1, device_id={"seq": mate}, device_id_type=MESH)

    @pl.when(above)
    def _():
        pl.semaphore_signal(barrier, inc=1, device_id={"dp": dp + 2}, device_id_type=MESH)

    @pl.when(below)
    def _():
        pl.semaphore_signal(barrier, inc=1, device_id={"dp": dp - 2}, device_id_type=MESH)

    pl.semaphore_wait(barrier, 2 + above.astype(jnp.int32) + below.astype(jnp.int32))

    def line(hop, up):
        origin = z - hop if up else z + hop
        source = piece_ref if hop == 0 else out_ref.at[origin, x, core]
        flow = 0 if up else 1
        return pltpu.make_async_remote_copy(
            src_ref=source, dst_ref=out_ref.at[origin, x, core],
            send_sem=line_send.at[flow, hop], recv_sem=line_recv.at[flow, hop],
            device_id={"dp": dp + 2 if up else dp - 2}, device_id_type=MESH,
        )

    def line_arrival(hop, up):
        origin = z - hop if up else z + hop
        flow = 0 if up else 1
        return pltpu.make_async_remote_copy(
            src_ref=piece_ref, dst_ref=out_ref.at[origin, x, core],
            send_sem=line_send.at[flow, hop - 1], recv_sem=line_recv.at[flow, hop - 1],
            device_id={"dp": dp + 2 if up else dp - 2}, device_id_type=MESH,
        )

    def side(step, origin, column):
        source = piece_ref if step == 0 else out_ref.at[origin, x, core]
        return pltpu.make_async_remote_copy(
            src_ref=source, dst_ref=out_ref.at[origin, column, core],
            send_sem=side_send.at[step], recv_sem=side_recv.at[step],
            device_id={"dp": 2 * z + 1 - x}, device_id_type=MESH,
        )

    def across(slot, origin, column, half):
        source = piece_ref if slot == 0 else out_ref.at[origin, column, core]
        return pltpu.make_async_remote_copy(
            src_ref=source, dst_ref=out_ref.at[origin, column, half],
            send_sem=core_send.at[slot], recv_sem=core_recv.at[slot],
            device_id={"seq": mate}, device_id_type=MESH,
        )

    waves = [(0, z, None)]
    for hop in range(1, count):
        waves.append((hop, z - hop, z >= hop))
        waves.append((count - 1 + hop, z + hop, z + hop < count))

    def guarded(condition, action):
        if condition is None:
            action()
        else:
            pl.when(condition)(action)

    keep = pltpu.make_async_copy(piece_ref, out_ref.at[z, x, core], local_sem)
    keep.start()
    pl.when(above)(lambda: line(0, True).start())
    pl.when(below)(lambda: line(0, False).start())
    side(0, z, x).start()
    across(0, z, x, core).start()

    def side_wave(step, origin):
        side(step, origin, 1 - x).wait_recv()
        across(steps + step, origin, 1 - x, core).start()

    for step, origin, condition in waves[1:]:
        up = step < count
        hop = step if up else step - count + 1

        def forward(step=step, origin=origin, up=up, hop=hop):
            line_arrival(hop, up).wait_recv()
            if hop < count - 1:
                pl.when(above if up else below)(lambda: line(hop, up).start())
            side(step, origin, x).start()
            across(step, origin, x, core).start()

        guarded(condition, forward)
        if not up:
            for late, place, holds in waves:
                late_hop = late if late < count else late - count + 1
                if late_hop == hop - 1:
                    guarded(holds, functools.partial(side_wave, late, place))
    for late, place, holds in waves[-2:]:
        guarded(holds, functools.partial(side_wave, late, place))

    keep.wait()
    for step, origin, condition in waves:
        def finish(step=step, origin=origin):
            side(step, origin, x).wait_send()
            across(step, origin, x, core).wait_send()
            across(steps + step, origin, 1 - x, core).wait_send()
            across(step, origin, x, 1 - core).wait_recv()
            across(steps + step, origin, 1 - x, 1 - core).wait_recv()
            up = step < count
            hop = step if up else step - count + 1
            if step == 0:
                pl.when(above)(lambda: line(0, True).wait_send())
                pl.when(below)(lambda: line(0, False).wait_send())
            elif hop < count - 1:
                pl.when(above if up else below)(lambda: line(hop, up).wait_send())

        guarded(condition, finish)


def gather_pieces(piece, count):
    steps = 2 * count - 1
    dma = pltpu.SemaphoreType.DMA
    return pl.pallas_call(
        gather_kernel,
        out_shape=jax.ShapeDtypeStruct((count, 2, 2) + piece.shape, piece.dtype),
        in_specs=[pl.BlockSpec(memory_space=pltpu.VMEM)],
        out_specs=pl.BlockSpec(memory_space=pltpu.VMEM),
        scratch_shapes=[
            dma((2, count)), dma((2, count)), dma((steps,)), dma((steps,)),
            dma((2 * steps,)), dma((2 * steps,)), dma(()),
        ],
        compiler_params=pltpu.CompilerParams(
            collective_id=0, has_side_effects=True, vmem_limit_bytes=24 * 2**20
        ),
        cost_estimate=pl.CostEstimate(
            flops=0, bytes_accessed=64 * piece.size * count, transcendentals=0
        ),
    )(piece)


def sum_kernel(chunks, factor, *refs):
    ins, outs = refs[:2], refs[2:4]
    beside, summed, lined = refs[4:6], refs[6:8], refs[8:10]
    side_send, side_recv, line_send, line_recv = refs[10:]
    count = ins[0].shape[0]
    dp = lax.axis_index("dp")
    z, x = dp // 2, dp % 2
    neighbour = 2 * z + 1 - x
    peers = [lax.rem(z + step, count) for step in range(1, count)]

    barrier = pltpu.get_barrier_semaphore()
    pl.semaphore_signal(barrier, inc=1, device_id={"dp": neighbour}, device_id_type=MESH)
    for peer in peers:
        pl.semaphore_signal(barrier, inc=1, device_id={"dp": 2 * peer + x}, device_id_type=MESH)
    pl.semaphore_wait(barrier, count)

    def rows_of(which, chunk):
        size = ins[which].shape[2] // chunks
        return pl.ds(chunk * size, size)

    def side(which, chunk):
        return pltpu.make_async_remote_copy(
            src_ref=ins[which].at[:, 1 - x, rows_of(which, chunk)],
            dst_ref=beside[which].at[chunk],
            send_sem=side_send.at[which, chunk], recv_sem=side_recv.at[which, chunk],
            device_id={"dp": neighbour}, device_id_type=MESH,
        )

    def line(which, chunk, step):
        peer = peers[step]
        return pltpu.make_async_remote_copy(
            src_ref=summed[which].at[chunk, peer],
            dst_ref=lined[which].at[chunk, step],
            send_sem=line_send.at[which, chunk, step], recv_sem=line_recv.at[which, chunk, step],
            device_id={"dp": 2 * peer + x}, device_id_type=MESH,
        )

    both = [(chunk, which) for chunk in range(chunks) for which in (0, 1)]
    for chunk, which in both:
        side(which, chunk).start()
    for chunk, which in both:
        side(which, chunk).wait_recv()
        for step in range(count - 1):
            peer = peers[step]
            summed[which][chunk, peer] = (
                ins[which][peer, x, rows_of(which, chunk)].astype(jnp.float32)
                + beside[which][chunk, peer].astype(jnp.float32)
            ).astype(jnp.bfloat16)
            line(which, chunk, step).start()
    for chunk, which in both:
        total = ins[which][z, x, rows_of(which, chunk)].astype(jnp.float32)
        total = total + beside[which][chunk, z].astype(jnp.float32)
        for step in range(count - 1):
            line(which, chunk, step).wait_recv()
            total = total + lined[which][chunk, step].astype(jnp.float32)
        outs[which][rows_of(which, chunk)] = total * factor
    for chunk, which in both:
        side(which, chunk).wait_send()
        for step in range(count - 1):
            line(which, chunk, step).wait_send()


def sum_tiles(arrays, count, chunks, factor):
    tiles = [a.reshape(count, 2, a.shape[0] // (2 * count), a.shape[1]) for a in arrays]
    vmem = pl.BlockSpec(memory_space=pltpu.VMEM)
    dma = pltpu.SemaphoreType.DMA

    def slots(lead):
        return [
            pltpu.VMEM((chunks, lead, t.shape[2] // chunks, t.shape[3]), t.dtype) for t in tiles
        ]

    return pl.pallas_call(
        functools.partial(sum_kernel, chunks, factor),
        out_shape=[jax.ShapeDtypeStruct(t.shape[2:], jnp.float32) for t in tiles],
        in_specs=[vmem, vmem],
        out_specs=[vmem, vmem],
        scratch_shapes=slots(count) + slots(count) + slots(count - 1) + [
            dma((2, chunks)), dma((2, chunks)),
            dma((2, chunks, count - 1)), dma((2, chunks, count - 1)),
        ],
        compiler_params=pltpu.CompilerParams(
            collective_id=1, has_side_effects=True, vmem_limit_bytes=24 * 2**20
        ),
        cost_estimate=pl.CostEstimate(
            flops=0, bytes_accessed=64 * tiles[0].size, transcendentals=0
        ),
    )(*tiles)


def head_body(frames, live, norm_gain, w_qkv, w_out, cotangent):
    length, width = frames.shape[1:]
    n_data = lax.axis_size("dp")
    n_seq = lax.axis_size("seq")
    me = lax.axis_index("seq")
    high, low = me // 2, me % 2
    shard = w_qkv.shape[0]
    inner = w_qkv.shape[1] // 3
    part = inner // 2
    score_scale = 1.0 / math.sqrt(HEAD_DIM)

    own_rows = lax.dynamic_slice_in_dim(w_qkv, low * (shard // 2), shard // 2, 0)
    choices = [
        jnp.concatenate(
            [own_rows[:, (2 * i + half) * part : (2 * i + half + 1) * part] for i in range(3)],
            axis=1,
        )
        for half in (0, 1)
    ]
    mine_qkv = jnp.where(high == 0, choices[0], choices[1])
    mine_out = lax.dynamic_slice_in_dim(w_out, low * (width // 2), width // 2, 1)
    packed_weights = jnp.concatenate([mine_out, mine_qkv], axis=1)

    upstream = cotangent[0]
    marks = jnp.zeros((16, width), jnp.bfloat16).at[0, :length].set(live[0].astype(jnp.bfloat16))
    packed = jnp.concatenate([frames[0], marks], axis=0)
    packs = [packed, swap(packed, 2), swap(packed, 1), swap(packed, 3)]
    cots = jnp.concatenate([upstream, swap(upstream, 2)], axis=0)
    rows = jnp.concatenate([pack[:length] for pack in packs], axis=0)
    key_live = jnp.concatenate([pack[length, :length] for pack in packs], axis=0)
    key_live = key_live.astype(jnp.float32)
    step = jnp.arange(length, dtype=jnp.float32)
    key_pos = jnp.concatenate(
        [step + ((me ^ flip) * length).astype(jnp.float32) for flip in (0, 2, 1, 3)]
    )
    queries = 2 * length
    query_live = key_live[:queries]

    unit_rows, inverse = norm_rows(rows.astype(jnp.float32))
    normed = (unit_rows * norm_gain).astype(jnp.bfloat16)

    gathered = gather_pieces(packed_weights, n_data // 2)
    part_qkv = gathered[..., width // 2 :].reshape(n_data * shard, 3 * part)
    halves = gathered[..., : width // 2].reshape(n_data, 2, shard // 2, width // 2)
    halves = lax.dynamic_slice_in_dim(halves, high * (n_data // 2), n_data // 2, 0)
    part_out = jnp.concatenate(
        [halves[:, half].reshape(part, width // 2) for half in (0, 1)], axis=1
    )

    def turned(weights, values):
        return lax.dot_general(
            weights, values, (((0,), (1,)), ((), ())), preferred_element_type=jnp.float32
        )

    query_t = turned(part_qkv[:, :part], normed[:queries]).astype(jnp.bfloat16)
    pairs_t = turned(part_qkv[:, part:], normed).astype(jnp.bfloat16)
    grad_t = (against(part_out, cots) * query_live[None, :]).astype(jnp.bfloat16)

    query_rows = jnp.stack([key_pos[:queries], query_live])
    att_t, dq_t, own_grads, other_grads = attend(
        query_t, grad_t, pairs_t[:part], pairs_t[part:],
        key_pos[:, None], key_live[:, None], query_rows, 2, score_scale,
    )
    block = width // n_seq
    other_grads = swap(other_grads, 1)
    partial_out = jnp.dot(att_t, cots, preferred_element_type=jnp.float32)
    other_grads, partial_out = lax.optimization_barrier((other_grads, partial_out))
    own_grads = own_grads + other_grads.astype(jnp.float32)

    grads_t = jnp.concatenate(
        [dq_t, own_grads.reshape(2 * part, queries).astype(jnp.bfloat16)], axis=0
    )
    unit = part // 2

    def units(start, count):
        return lax.dynamic_slice_in_dim(grads_t, start * unit, count * unit, 0)

    beside = swap(units(2 * (high + 1 - low), 2), 1)
    facing = swap(units(4 * (1 - high) + low, 1), 2)
    corner = swap(units(4 * (1 - high) + 1 - low, 1), 3)

    def columns_of(flip):
        return lax.dynamic_slice_in_dim(partial_out, (me ^ flip) * block, block, 1)

    columns = [swap(columns_of(flip).astype(jnp.bfloat16), flip) for flip in (1, 2, 3)]
    two = jnp.concatenate([units(2 * (high + low), 2), beside], axis=1)
    one = jnp.concatenate(
        [facing[:, length:], facing[:, :length], corner[:, length:], corner[:, :length]], axis=1
    )
    first = low == 0
    keep_t = jnp.where(
        first, jnp.concatenate([two, one], axis=0), jnp.concatenate([one, two], axis=0)
    )
    keep_t, late_t = lax.optimization_barrier((keep_t, grads_t))
    sum_qkv = lax.dot_general(
        normed, keep_t, (((0,), (1,)), ((), ())), preferred_element_type=jnp.float32
    )

    columns = [value.astype(jnp.float32) for value in columns]
    same, across = columns_of(0) + columns[0], columns[1] + columns[2]
    sum_out = jnp.concatenate(
        [jnp.where(high == 0, same, across), jnp.where(high == 0, across, same)], axis=0
    )

    def through_weights(piece):
        return lax.dot_general(
            piece, part_qkv, (((0,), (1,)), ((), ())), preferred_element_type=jnp.float32
        )

    sent = through_weights(late_t[:, length:]).astype(jnp.bfloat16)
    sent, sum_qkv = lax.optimization_barrier((sent, sum_qkv.astype(jnp.bfloat16)))
    arrived = swap(sent, 2)
    factor = 1.0 / math.sqrt(n_data * n_seq * length)
    tile_qkv, tile_out = sum_tiles(
        [sum_qkv, sum_out.astype(jnp.bfloat16)], n_data // 2, 5, factor
    )
    grad_unit = through_weights(late_t[:, :length]) + arrived.astype(jnp.float32)
    grad_unit = grad_unit * norm_gain
    own_unit = unit_rows[:length]
    through = inverse[:length] * (
        grad_unit
        - jnp.mean(grad_unit, axis=-1, keepdims=True)
        - own_unit * jnp.mean(grad_unit * own_unit, axis=-1, keepdims=True)
    )
    grad_rows = (upstream.astype(jnp.float32) + through).astype(jnp.bfloat16)[None]

    return (grad_rows, tile_qkv, tile_out)


def solution(mesh):
    n_seq = mesh.shape["seq"]

    def whole(frames, live, norm_gain, w_qkv, w_out, cotangent):
        heads_fit = n_seq == 4 and mesh.shape["dp"] == 8 and frames.shape[1] <= frames.shape[1] // n_seq + 2 * WIN
        chosen = head_body if heads_fit else body
        return split(chosen, mesh)(frames, live, norm_gain, w_qkv, w_out, cotangent)

    return whole


def split(chosen, mesh):
    return jax.shard_map(
        chosen,
        mesh=mesh,
        in_specs=(
            P("dp", "seq", None),
            P("dp", "seq"),
            P(),
            P("dp", None),
            P("dp", None),
            P("dp", "seq", None),
        ),
        out_specs=(P("dp", "seq", None), P("dp", "seq"), P("dp", "seq")),
        check_vma=False,
    )
```

```python
import functools
import math

import jax
import jax.numpy as jnp
from jax import lax
from jax.experimental import pallas as pl
from jax.experimental.pallas import tpu as pltpu
from jax.sharding import PartitionSpec as P

HEAD_DIM = 64
WIN = 512


EPS = 1e-05
NEG = -1e30


def from_behind(value, axis, steps):
    count = lax.axis_size(axis)
    leading, last = (max(0, -steps), min(count, count - steps))
    return lax.ppermute(value, axis, [(source, source + steps) for source in range(leading, last)])


def norm_rows(values_in):
    average = jnp.mean(values_in, axis=-1, keepdims=True)
    centred = values_in - average
    inverse = lax.rsqrt(jnp.mean(centred * centred, axis=-1, keepdims=True) + EPS)
    return (centred * inverse, inverse)


def against(left, right):
    return lax.dot_general(
        left, right, (((1,), (1,)), ((), ())), preferred_element_type=jnp.float32
    )


def leading(left, right):
    return lax.dot_general(
        left, right, (((0,), (0,)), ((), ())), preferred_element_type=jnp.float32
    )


def head_terms(query_head, key_head, value_head, grad_head, allowed, query_live, score_scale):
    scores = jnp.where(allowed, against(query_head, key_head) * score_scale, NEG)
    row_peak = jnp.max(scores, axis=-1, keepdims=True)
    exponent = jnp.exp(scores - row_peak)
    probabilities = exponent / jnp.sum(exponent, axis=-1, keepdims=True)
    probs_b = probabilities.astype(jnp.bfloat16)
    mixed = jnp.dot(probs_b, value_head, preferred_element_type=jnp.float32) * query_live[:, None]
    attended = mixed.astype(jnp.bfloat16)
    row_delta = jnp.sum(grad_head.astype(jnp.float32) * attended.astype(jnp.float32), axis=1)
    grad_probs = against(grad_head, value_head)
    grad_scores = (probabilities * (grad_probs - row_delta[:, None]) * score_scale).astype(
        jnp.bfloat16
    )
    grad_query = jnp.dot(grad_scores, key_head, preferred_element_type=jnp.float32)
    grad_key = leading(grad_scores, query_head)
    grad_value = leading(probs_b, grad_head)
    return (attended, grad_query, grad_key, grad_value)


def body(frames, live, norm_gain, w_qkv, w_out, cotangent):
    length = frames.shape[1]
    n_data = lax.axis_size("dp")
    n_seq = lax.axis_size("seq")
    full_qkv, full_out = (
        lax.all_gather(w_qkv, "dp", axis=0, tiled=True),
        lax.all_gather(w_out, "dp", axis=0, tiled=True),
    )
    inner = full_out.shape[0]
    heads = inner // HEAD_DIM
    hidden = frames[0].astype(jnp.float32)
    unit_rows, inverse = norm_rows(hidden)
    normed = (unit_rows * norm_gain).astype(jnp.bfloat16)
    projected = jnp.dot(normed, full_qkv, preferred_element_type=jnp.float32).astype(jnp.bfloat16)
    query = projected[:, :inner]
    key_values = projected[:, inner:]
    live_row = live[0]
    query_live = live_row.astype(jnp.float32)
    live_mark = live_row.astype(jnp.bfloat16)
    upstream = cotangent[0]
    grad_att = (against(upstream, full_out) * query_live[:, None]).astype(jnp.bfloat16)
    neighbours = -(-WIN // length)
    offsets = list(range(neighbours, 0, -1)) + list(range(-1, -neighbours - 1, -1))
    before_pairs, before_marks, after_pairs, after_marks = ([], [], [], [])
    for offset in offsets:
        distance = abs(offset)
        row_count = min(length, WIN - (distance - 1) * length)
        if offset > 0:
            send_pairs = key_values
            send_marks = live_mark
        else:
            send_pairs = key_values
            send_marks = live_mark
        got_pairs, got_marks = from_behind((send_pairs, send_marks), "seq", offset)
        if offset > 0:
            before_pairs.append(got_pairs)
            before_marks.append(got_marks)
        else:
            after_pairs.append(got_pairs)
            after_marks.append(got_marks)
    ext_pairs = jnp.concatenate(before_pairs + [key_values] + after_pairs, axis=0)
    ext_live = jnp.concatenate(before_marks + [live_mark] + after_marks, axis=0).astype(jnp.float32)
    total_span = length + 2 * WIN
    block_rows = min(length, 512)
    key_span = block_rows + 2 * WIN
    query_pos = jnp.arange(block_rows, dtype=jnp.int32)
    key_pos = jnp.arange(key_span, dtype=jnp.int32) - WIN
    in_window = jnp.abs(query_pos[:, None] - key_pos[None, :]) <= WIN
    allowances = [in_window & (ext_live[None, :] > 0.5)]
    score_scale = 1.0 / math.sqrt(HEAD_DIM)

    def split_heads(matrix):
        return matrix.reshape(matrix.shape[0], heads, HEAD_DIM).transpose(1, 0, 2)

    def merge_heads(matrix):
        return matrix.transpose(1, 0, 2).reshape(matrix.shape[1], inner)

    def one_head(inputs):
        query_head, key_head, value_head, grad_head = inputs
        out_blocks, query_blocks = ([], [])
        key_grads = jnp.zeros((total_span, HEAD_DIM), jnp.float32)
        value_grads = jnp.zeros((total_span, HEAD_DIM), jnp.float32)
        attended, grad_query, grad_key, grad_value = head_terms(
            query_head, key_head, value_head, grad_head, allowances[0], query_live, score_scale
        )
        out_blocks.append(attended)
        query_blocks.append(grad_query)
        key_grads = key_grads.at[0:key_span].add(grad_key)
        value_grads = value_grads.at[0:key_span].add(grad_value)
        return (
            jnp.concatenate(out_blocks, axis=0),
            jnp.concatenate(query_blocks, axis=0),
            key_grads,
            value_grads,
        )

    att_heads, query_heads, key_heads, value_heads = lax.map(
        one_head,
        (
            split_heads(query),
            split_heads(ext_pairs[:, :inner]),
            split_heads(ext_pairs[:, inner:]),
            split_heads(grad_att),
        ),
    )
    attention = merge_heads(att_heads)
    grad_query = merge_heads(query_heads)
    ext_grads = jnp.concatenate([merge_heads(key_heads), merge_heads(value_heads)], axis=1)
    own_grads = ext_grads[WIN : WIN + length]
    for offset in offsets:
        distance = abs(offset)
        row_count = min(length, WIN - (distance - 1) * length)
        if offset > 0:
            first_row = WIN - distance * length + length - row_count
        else:
            first_row = WIN + length + (distance - 1) * length
        arrived = from_behind(ext_grads[first_row : first_row + row_count], "seq", -offset)
        if offset > 0:
            own_grads = own_grads.at[length - row_count :].add(arrived)
        else:
            own_grads = own_grads.at[:row_count].add(arrived)
    grad_projected = jnp.concatenate([grad_query, own_grads], axis=1).astype(jnp.bfloat16)
    grad_unit = against(grad_projected, full_qkv) * norm_gain
    through = inverse * (
        grad_unit
        - jnp.mean(grad_unit, axis=-1, keepdims=True)
        - unit_rows * jnp.mean(grad_unit * unit_rows, axis=-1, keepdims=True)
    )
    grad_rows = (upstream.astype(jnp.float32) + through).astype(jnp.bfloat16)[None]
    factor = 1.0 / math.sqrt(n_data * n_seq * length)

    def blocked(left, right):
        left_tiles = left.reshape(length, n_data, left.shape[1] // n_data)
        right_tiles = right.reshape(length, n_seq, right.shape[1] // n_seq)
        tile_grid = jnp.einsum(
            "fpr,fsc->psrc", left_tiles, right_tiles, preferred_element_type=jnp.float32
        )
        return tile_grid.reshape(n_data * n_seq * left_tiles.shape[2], right_tiles.shape[2])

    sum_qkv, sum_out = (
        lax.psum_scatter(
            blocked(normed, grad_projected), ("dp", "seq"), scatter_dimension=0, tiled=True
        ),
        lax.psum_scatter(
            blocked(attention, upstream), ("dp", "seq"), scatter_dimension=0, tiled=True
        ),
    )
    return (grad_rows, sum_qkv * factor, sum_out * factor)


def swap(value, flip):
    count = lax.axis_size("seq")
    return lax.ppermute(value, "seq", [(source, source ^ flip) for source in range(count)])


def attend_kernel(score_scale, blocks, q_ref, g_ref, k_ref, v_ref, ends_ref, live_ref, qlive_ref,
                  att_ref, dq_ref, own_ref, other_ref, bias_ref):
    rows = q_ref.shape[1] // blocks
    span = k_ref.shape[1]

    @pl.when(pl.program_id(0) == 0)
    def _():
        for block in range(blocks):
            columns = slice(block * rows, (block + 1) * rows)
            near = jnp.abs(ends_ref[...] - qlive_ref[0:1, columns]) <= WIN
            bias_ref[:, columns] = jnp.where(near & (live_ref[...] > 0.5), 0.0, NEG)

    key_t, value_t = k_ref[...], v_ref[...]
    key = key_t.T
    value = value_t.T
    key_grad = jnp.zeros((span, HEAD_DIM), jnp.float32)
    value_grad = jnp.zeros((span, HEAD_DIM), jnp.float32)
    for block in range(blocks):
        columns = slice(block * rows, (block + 1) * rows)
        query_t, grad_t = q_ref[:, columns], g_ref[:, columns]
        scores = jnp.dot(
            key, (query_t * score_scale).astype(jnp.bfloat16), preferred_element_type=jnp.float32
        )
        scores = scores + bias_ref[:, columns]
        exponent = jnp.exp(scores - jnp.max(scores, axis=0, keepdims=True))
        inverse = 1.0 / jnp.sum(exponent, axis=0, keepdims=True)
        probabilities = exponent * inverse
        probs_b = probabilities.astype(jnp.bfloat16)
        mixed = jnp.dot(value_t, probs_b, preferred_element_type=jnp.float32)
        attended = (mixed * qlive_ref[1:2, columns]).astype(jnp.bfloat16)
        att_ref[:, columns] = attended
        row_delta = jnp.sum(
            grad_t.astype(jnp.float32) * attended.astype(jnp.float32), axis=0, keepdims=True
        )
        grad_probs = jnp.dot(
            value, (grad_t * score_scale).astype(jnp.bfloat16), preferred_element_type=jnp.float32
        )
        grad_scores = (probabilities * (grad_probs - row_delta * score_scale)).astype(
            jnp.bfloat16
        )
        dq_ref[:, columns] = jnp.dot(
            key_t, grad_scores, preferred_element_type=jnp.float32
        ).astype(jnp.bfloat16)
        key_grad += against(grad_scores, query_t)
        value_grad += against(probs_b, grad_t)
    half = span // 2
    key_grad_t, value_grad_t = key_grad.T, value_grad.T
    own_ref[0] = key_grad_t[:, :half]
    own_ref[1] = value_grad_t[:, :half]
    other_ref[0] = key_grad_t[:, half:].astype(jnp.bfloat16)
    other_ref[1] = value_grad_t[:, half:].astype(jnp.bfloat16)


def attend(query_t, grad_t, key_t, value_t, key_pos, key_live, query_rows, blocks, score_scale):
    features, queries = query_t.shape
    span = key_t.shape[1]
    half = span // 2
    heads = features // HEAD_DIM
    by_query = pl.BlockSpec((HEAD_DIM, queries), lambda h: (h, 0))
    by_key = pl.BlockSpec((HEAD_DIM, span), lambda h: (h, 0))
    grads = pl.BlockSpec((2, HEAD_DIM, half), lambda h: (0, h, 0))
    return pl.pallas_call(
        functools.partial(attend_kernel, score_scale, blocks),
        grid=(heads,),
        in_specs=[
            by_query,
            by_query,
            by_key,
            by_key,
            pl.BlockSpec((span, 1), lambda h: (0, 0)),
            pl.BlockSpec((span, 1), lambda h: (0, 0)),
            pl.BlockSpec((2, queries), lambda h: (0, 0)),
        ],
        out_specs=[by_query, by_query, grads, grads],
        out_shape=[
            jax.ShapeDtypeStruct((features, queries), jnp.bfloat16),
            jax.ShapeDtypeStruct((features, queries), jnp.bfloat16),
            jax.ShapeDtypeStruct((2, features, half), jnp.float32),
            jax.ShapeDtypeStruct((2, features, half), jnp.bfloat16),
        ],
        scratch_shapes=[pltpu.VMEM((span, queries), jnp.float32)],
        compiler_params=pltpu.CompilerParams(vmem_limit_bytes=40 * 2**20),
        cost_estimate=pl.CostEstimate(
            flops=10 * features * queries * span,
            bytes_accessed=12 * features * span,
            transcendentals=heads * queries * span,
        ),
    )(query_t, grad_t, key_t, value_t, key_pos, key_live, query_rows)


MESH = pl.DeviceIdType.MESH


def gather_kernel(piece_ref, out_ref, line_send, line_recv, side_send, side_recv,
                  core_send, core_recv, local_sem):
    count = out_ref.shape[0]
    dp, seq = lax.axis_index("dp"), lax.axis_index("seq")
    z, x, core = dp // 2, dp % 2, seq % 2
    mate = seq + 1 - 2 * core
    steps = 2 * count - 1
    above, below = z < count - 1, z > 0

    barrier = pltpu.get_barrier_semaphore()
    pl.semaphore_signal(barrier, inc=1, device_id={"dp": 2 * z + 1 - x}, device_id_type=MESH)
    pl.semaphore_signal(barrier, inc=1, device_id={"seq": mate}, device_id_type=MESH)

    @pl.when(above)
    def _():
        pl.semaphore_signal(barrier, inc=1, device_id={"dp": dp + 2}, device_id_type=MESH)

    @pl.when(below)
    def _():
        pl.semaphore_signal(barrier, inc=1, device_id={"dp": dp - 2}, device_id_type=MESH)

    pl.semaphore_wait(barrier, 2 + above.astype(jnp.int32) + below.astype(jnp.int32))

    def line(hop, up):
        origin = z - hop if up else z + hop
        source = piece_ref if hop == 0 else out_ref.at[origin, x, core]
        flow = 0 if up else 1
        return pltpu.make_async_remote_copy(
            src_ref=source, dst_ref=out_ref.at[origin, x, core],
            send_sem=line_send.at[flow, hop], recv_sem=line_recv.at[flow, hop],
            device_id={"dp": dp + 2 if up else dp - 2}, device_id_type=MESH,
        )

    def line_arrival(hop, up):
        origin = z - hop if up else z + hop
        flow = 0 if up else 1
        return pltpu.make_async_remote_copy(
            src_ref=piece_ref, dst_ref=out_ref.at[origin, x, core],
            send_sem=line_send.at[flow, hop - 1], recv_sem=line_recv.at[flow, hop - 1],
            device_id={"dp": dp + 2 if up else dp - 2}, device_id_type=MESH,
        )

    def side(step, origin, column):
        source = piece_ref if step == 0 else out_ref.at[origin, x, core]
        return pltpu.make_async_remote_copy(
            src_ref=source, dst_ref=out_ref.at[origin, column, core],
            send_sem=side_send.at[step], recv_sem=side_recv.at[step],
            device_id={"dp": 2 * z + 1 - x}, device_id_type=MESH,
        )

    def across(slot, origin, column, half):
        source = piece_ref if slot == 0 else out_ref.at[origin, column, core]
        return pltpu.make_async_remote_copy(
            src_ref=source, dst_ref=out_ref.at[origin, column, half],
            send_sem=core_send.at[slot], recv_sem=core_recv.at[slot],
            device_id={"seq": mate}, device_id_type=MESH,
        )

    waves = [(0, z, None)]
    for hop in range(1, count):
        waves.append((hop, z - hop, z >= hop))
        waves.append((count - 1 + hop, z + hop, z + hop < count))

    def guarded(condition, action):
        if condition is None:
            action()
        else:
            pl.when(condition)(action)

    keep = pltpu.make_async_copy(piece_ref, out_ref.at[z, x, core], local_sem)
    keep.start()
    pl.when(above)(lambda: line(0, True).start())
    pl.when(below)(lambda: line(0, False).start())
    side(0, z, x).start()
    across(0, z, x, core).start()

    def side_wave(step, origin):
        side(step, origin, 1 - x).wait_recv()
        across(steps + step, origin, 1 - x, core).start()

    for step, origin, condition in waves[1:]:
        up = step < count
        hop = step if up else step - count + 1

        def forward(step=step, origin=origin, up=up, hop=hop):
            line_arrival(hop, up).wait_recv()
            if hop < count - 1:
                pl.when(above if up else below)(lambda: line(hop, up).start())
            side(step, origin, x).start()
            across(step, origin, x, core).start()

        guarded(condition, forward)
        if not up:
            for late, place, holds in waves:
                late_hop = late if late < count else late - count + 1
                if late_hop == hop - 1:
                    guarded(holds, functools.partial(side_wave, late, place))
    for late, place, holds in waves[-2:]:
        guarded(holds, functools.partial(side_wave, late, place))

    keep.wait()
    for step, origin, condition in waves:
        def finish(step=step, origin=origin):
            side(step, origin, x).wait_send()
            across(step, origin, x, core).wait_send()
            across(steps + step, origin, 1 - x, core).wait_send()
            across(step, origin, x, 1 - core).wait_recv()
            across(steps + step, origin, 1 - x, 1 - core).wait_recv()
            up = step < count
            hop = step if up else step - count + 1
            if step == 0:
                pl.when(above)(lambda: line(0, True).wait_send())
                pl.when(below)(lambda: line(0, False).wait_send())
            elif hop < count - 1:
                pl.when(above if up else below)(lambda: line(hop, up).wait_send())

        guarded(condition, finish)


def gather_pieces(piece, count):
    steps = 2 * count - 1
    dma = pltpu.SemaphoreType.DMA
    return pl.pallas_call(
        gather_kernel,
        out_shape=jax.ShapeDtypeStruct((count, 2, 2) + piece.shape, piece.dtype),
        in_specs=[pl.BlockSpec(memory_space=pltpu.VMEM)],
        out_specs=pl.BlockSpec(memory_space=pltpu.VMEM),
        scratch_shapes=[
            dma((2, count)), dma((2, count)), dma((steps,)), dma((steps,)),
            dma((2 * steps,)), dma((2 * steps,)), dma(()),
        ],
        compiler_params=pltpu.CompilerParams(
            collective_id=0, has_side_effects=True, vmem_limit_bytes=24 * 2**20
        ),
        cost_estimate=pl.CostEstimate(
            flops=0, bytes_accessed=64 * piece.size * count, transcendentals=0
        ),
    )(piece)


def sum_kernel(chunks, factor, *refs):
    ins, outs = refs[:2], refs[2:4]
    beside, summed, lined = refs[4:6], refs[6:8], refs[8:10]
    side_send, side_recv, line_send, line_recv = refs[10:]
    count = ins[0].shape[0]
    dp = lax.axis_index("dp")
    z, x = dp // 2, dp % 2
    neighbour = 2 * z + 1 - x
    peers = [lax.rem(z + step, count) for step in range(1, count)]

    barrier = pltpu.get_barrier_semaphore()
    pl.semaphore_signal(barrier, inc=1, device_id={"dp": neighbour}, device_id_type=MESH)
    for peer in peers:
        pl.semaphore_signal(barrier, inc=1, device_id={"dp": 2 * peer + x}, device_id_type=MESH)
    pl.semaphore_wait(barrier, count)

    def rows_of(which, chunk):
        size = ins[which].shape[2] // chunks
        return pl.ds(chunk * size, size)

    def side(which, chunk):
        return pltpu.make_async_remote_copy(
            src_ref=ins[which].at[:, 1 - x, rows_of(which, chunk)],
            dst_ref=beside[which].at[chunk],
            send_sem=side_send.at[which, chunk], recv_sem=side_recv.at[which, chunk],
            device_id={"dp": neighbour}, device_id_type=MESH,
        )

    def line(which, chunk, step):
        peer = peers[step]
        return pltpu.make_async_remote_copy(
            src_ref=summed[which].at[chunk, peer],
            dst_ref=lined[which].at[chunk, step],
            send_sem=line_send.at[which, chunk, step], recv_sem=line_recv.at[which, chunk, step],
            device_id={"dp": 2 * peer + x}, device_id_type=MESH,
        )

    both = [(chunk, which) for chunk in range(chunks) for which in (0, 1)]
    for chunk, which in both:
        side(which, chunk).start()
    for chunk, which in both:
        side(which, chunk).wait_recv()
        for step in range(count - 1):
            peer = peers[step]
            summed[which][chunk, peer] = (
                ins[which][peer, x, rows_of(which, chunk)].astype(jnp.float32)
                + beside[which][chunk, peer].astype(jnp.float32)
            ).astype(jnp.bfloat16)
            line(which, chunk, step).start()
    for chunk, which in both:
        total = ins[which][z, x, rows_of(which, chunk)].astype(jnp.float32)
        total = total + beside[which][chunk, z].astype(jnp.float32)
        for step in range(count - 1):
            line(which, chunk, step).wait_recv()
            total = total + lined[which][chunk, step].astype(jnp.float32)
        outs[which][rows_of(which, chunk)] = total * factor
    for chunk, which in both:
        side(which, chunk).wait_send()
        for step in range(count - 1):
            line(which, chunk, step).wait_send()


def sum_tiles(arrays, count, chunks, factor):
    tiles = [a.reshape(count, 2, a.shape[0] // (2 * count), a.shape[1]) for a in arrays]
    vmem = pl.BlockSpec(memory_space=pltpu.VMEM)
    dma = pltpu.SemaphoreType.DMA

    def slots(lead):
        return [
            pltpu.VMEM((chunks, lead, t.shape[2] // chunks, t.shape[3]), t.dtype) for t in tiles
        ]

    return pl.pallas_call(
        functools.partial(sum_kernel, chunks, factor),
        out_shape=[jax.ShapeDtypeStruct(t.shape[2:], jnp.float32) for t in tiles],
        in_specs=[vmem, vmem],
        out_specs=[vmem, vmem],
        scratch_shapes=slots(count) + slots(count) + slots(count - 1) + [
            dma((2, chunks)), dma((2, chunks)),
            dma((2, chunks, count - 1)), dma((2, chunks, count - 1)),
        ],
        compiler_params=pltpu.CompilerParams(
            collective_id=1, has_side_effects=True, vmem_limit_bytes=24 * 2**20
        ),
        cost_estimate=pl.CostEstimate(
            flops=0, bytes_accessed=64 * tiles[0].size, transcendentals=0
        ),
    )(*tiles)


def assemble_kernel(two_ref, beside_ref, facing_ref, corner_ref, out_ref):
    low = lax.axis_index("seq") % 2
    queries = two_ref.shape[1]
    length, unit = queries // 2, facing_ref.shape[0]

    def place(two_row, one_row):
        out_ref[two_row : two_row + 2 * unit, :queries] = two_ref[...]
        out_ref[two_row : two_row + 2 * unit, queries:] = beside_ref[...]
        rows = slice(one_row, one_row + unit)
        for start, piece in ((0, facing_ref), (queries, corner_ref)):
            out_ref[rows, start : start + length] = piece[:, length:]
            out_ref[rows, start + length : start + queries] = piece[:, :length]

    pl.when(low == 0)(lambda: place(0, 2 * unit))
    pl.when(low == 1)(lambda: place(unit, 0))


def assemble(two, beside, facing, corner):
    vmem = pl.BlockSpec(memory_space=pltpu.VMEM)
    rows, queries = two.shape
    return pl.pallas_call(
        assemble_kernel,
        out_shape=jax.ShapeDtypeStruct((rows + facing.shape[0], 2 * queries), two.dtype),
        in_specs=[vmem] * 4,
        out_specs=vmem,
        compiler_params=pltpu.CompilerParams(vmem_limit_bytes=16 * 2**20),
        cost_estimate=pl.CostEstimate(flops=0, bytes_accessed=8 * two.size, transcendentals=0),
    )(two, beside, facing, corner)


def head_body(frames, live, norm_gain, w_qkv, w_out, cotangent):
    length, width = frames.shape[1:]
    n_data = lax.axis_size("dp")
    n_seq = lax.axis_size("seq")
    me = lax.axis_index("seq")
    high, low = me // 2, me % 2
    shard = w_qkv.shape[0]
    inner = w_qkv.shape[1] // 3
    part = inner // 2
    score_scale = 1.0 / math.sqrt(HEAD_DIM)

    own_rows = lax.dynamic_slice_in_dim(w_qkv, low * (shard // 2), shard // 2, 0)
    choices = [
        jnp.concatenate(
            [own_rows[:, (2 * i + half) * part : (2 * i + half + 1) * part] for i in range(3)],
            axis=1,
        )
        for half in (0, 1)
    ]
    mine_qkv = jnp.where(high == 0, choices[0], choices[1])
    mine_out = lax.dynamic_slice_in_dim(w_out, low * (width // 2), width // 2, 1)
    packed_weights = jnp.concatenate([mine_out, mine_qkv], axis=1)

    upstream = cotangent[0]
    marks = jnp.zeros((16, width), jnp.bfloat16).at[0, :length].set(live[0].astype(jnp.bfloat16))
    packed = jnp.concatenate([frames[0], marks], axis=0)
    packs = [packed, swap(packed, 2), swap(packed, 1), swap(packed, 3)]
    cots = jnp.concatenate([upstream, swap(upstream, 2)], axis=0)
    rows = jnp.concatenate([pack[:length] for pack in packs], axis=0)
    key_live = jnp.concatenate([pack[length, :length] for pack in packs], axis=0)
    key_live = key_live.astype(jnp.float32)
    step = jnp.arange(length, dtype=jnp.float32)
    key_pos = jnp.concatenate(
        [step + ((me ^ flip) * length).astype(jnp.float32) for flip in (0, 2, 1, 3)]
    )
    queries = 2 * length
    query_live = key_live[:queries]

    unit_rows, inverse = norm_rows(rows.astype(jnp.float32))
    normed = (unit_rows * norm_gain).astype(jnp.bfloat16)

    gathered = gather_pieces(packed_weights, n_data // 2)
    part_qkv = gathered[..., width // 2 :].reshape(n_data * shard, 3 * part)
    halves = gathered[..., : width // 2].reshape(n_data, 2, shard // 2, width // 2)
    halves = lax.dynamic_slice_in_dim(halves, high * (n_data // 2), n_data // 2, 0)
    part_out = jnp.concatenate(
        [halves[:, half].reshape(part, width // 2) for half in (0, 1)], axis=1
    )

    def turned(weights, values):
        return lax.dot_general(
            weights, values, (((0,), (1,)), ((), ())), preferred_element_type=jnp.float32
        )

    query_t = turned(part_qkv[:, :part], normed[:queries]).astype(jnp.bfloat16)
    pairs_t = turned(part_qkv[:, part:], normed).astype(jnp.bfloat16)
    grad_t = (against(part_out, cots) * query_live[None, :]).astype(jnp.bfloat16)

    query_rows = jnp.stack([key_pos[:queries], query_live])
    att_t, dq_t, own_grads, other_grads = attend(
        query_t, grad_t, pairs_t[:part], pairs_t[part:],
        key_pos[:, None], key_live[:, None], query_rows, 2, score_scale,
    )
    block = width // n_seq
    other_grads = swap(other_grads, 1)
    partial_out = jnp.dot(att_t, cots, preferred_element_type=jnp.float32)
    other_grads, partial_out = lax.optimization_barrier((other_grads, partial_out))
    own_grads = own_grads + other_grads.astype(jnp.float32)

    grads_t = jnp.concatenate(
        [dq_t, own_grads.reshape(2 * part, queries).astype(jnp.bfloat16)], axis=0
    )
    unit = part // 2

    def units(start, count):
        return lax.dynamic_slice_in_dim(grads_t, start * unit, count * unit, 0)

    beside = swap(units(2 * (high + 1 - low), 2), 1)
    facing = swap(units(4 * (1 - high) + low, 1), 2)
    corner = swap(units(4 * (1 - high) + 1 - low, 1), 3)

    def columns_of(flip):
        return lax.dynamic_slice_in_dim(partial_out, (me ^ flip) * block, block, 1)

    columns = [swap(columns_of(flip).astype(jnp.bfloat16), flip) for flip in (1, 2, 3)]
    keep_t = assemble(units(2 * (high + low), 2), beside, facing, corner)
    keep_t, late_t, columns = lax.optimization_barrier((keep_t, grads_t, columns))
    sum_qkv = lax.dot_general(
        normed, keep_t, (((0,), (1,)), ((), ())), preferred_element_type=jnp.float32
    )

    columns = [value.astype(jnp.float32) for value in columns]
    same, across = columns_of(0) + columns[0], columns[1] + columns[2]
    sum_out = jnp.concatenate(
        [jnp.where(high == 0, same, across), jnp.where(high == 0, across, same)], axis=0
    )

    def through_weights(piece):
        return lax.dot_general(
            piece, part_qkv, (((0,), (1,)), ((), ())), preferred_element_type=jnp.float32
        )

    sent = through_weights(late_t[:, length:]).astype(jnp.bfloat16)
    sent, sum_qkv = lax.optimization_barrier((sent, sum_qkv.astype(jnp.bfloat16)))
    arrived = swap(sent, 2)
    factor = 1.0 / math.sqrt(n_data * n_seq * length)
    tile_qkv, tile_out = sum_tiles(
        [sum_qkv, sum_out.astype(jnp.bfloat16)], n_data // 2, 5, factor
    )
    grad_unit = through_weights(late_t[:, :length]) + arrived.astype(jnp.float32)
    grad_unit = grad_unit * norm_gain
    own_unit = unit_rows[:length]
    through = inverse[:length] * (
        grad_unit
        - jnp.mean(grad_unit, axis=-1, keepdims=True)
        - own_unit * jnp.mean(grad_unit * own_unit, axis=-1, keepdims=True)
    )
    grad_rows = (upstream.astype(jnp.float32) + through).astype(jnp.bfloat16)[None]

    return (grad_rows, tile_qkv, tile_out)


def solution(mesh):
    n_seq = mesh.shape["seq"]

    def whole(frames, live, norm_gain, w_qkv, w_out, cotangent):
        heads_fit = n_seq == 4 and mesh.shape["dp"] == 8 and frames.shape[1] <= frames.shape[1] // n_seq + 2 * WIN
        chosen = head_body if heads_fit else body
        return split(chosen, mesh)(frames, live, norm_gain, w_qkv, w_out, cotangent)

    return whole


def split(chosen, mesh):
    return jax.shard_map(
        chosen,
        mesh=mesh,
        in_specs=(
            P("dp", "seq", None),
            P("dp", "seq"),
            P(),
            P("dp", None),
            P("dp", None),
            P("dp", "seq", None),
        ),
        out_specs=(P("dp", "seq", None), P("dp", "seq"), P("dp", "seq")),
        check_vma=False,
    )
```

```python
import functools
import math

import jax
import jax.numpy as jnp
from jax import lax
from jax.experimental import pallas as pl
from jax.experimental.pallas import tpu as pltpu
from jax.sharding import PartitionSpec as P

HEAD_DIM = 64
WIN = 512


EPS = 1e-05
NEG = -1e30


def from_behind(value, axis, steps):
    count = lax.axis_size(axis)
    leading, last = (max(0, -steps), min(count, count - steps))
    return lax.ppermute(value, axis, [(source, source + steps) for source in range(leading, last)])


def norm_rows(values_in):
    average = jnp.mean(values_in, axis=-1, keepdims=True)
    centred = values_in - average
    inverse = lax.rsqrt(jnp.mean(centred * centred, axis=-1, keepdims=True) + EPS)
    return (centred * inverse, inverse)


def against(left, right):
    return lax.dot_general(
        left, right, (((1,), (1,)), ((), ())), preferred_element_type=jnp.float32
    )


def leading(left, right):
    return lax.dot_general(
        left, right, (((0,), (0,)), ((), ())), preferred_element_type=jnp.float32
    )


def head_terms(query_head, key_head, value_head, grad_head, allowed, query_live, score_scale):
    scores = jnp.where(allowed, against(query_head, key_head) * score_scale, NEG)
    row_peak = jnp.max(scores, axis=-1, keepdims=True)
    exponent = jnp.exp(scores - row_peak)
    probabilities = exponent / jnp.sum(exponent, axis=-1, keepdims=True)
    probs_b = probabilities.astype(jnp.bfloat16)
    mixed = jnp.dot(probs_b, value_head, preferred_element_type=jnp.float32) * query_live[:, None]
    attended = mixed.astype(jnp.bfloat16)
    row_delta = jnp.sum(grad_head.astype(jnp.float32) * attended.astype(jnp.float32), axis=1)
    grad_probs = against(grad_head, value_head)
    grad_scores = (probabilities * (grad_probs - row_delta[:, None]) * score_scale).astype(
        jnp.bfloat16
    )
    grad_query = jnp.dot(grad_scores, key_head, preferred_element_type=jnp.float32)
    grad_key = leading(grad_scores, query_head)
    grad_value = leading(probs_b, grad_head)
    return (attended, grad_query, grad_key, grad_value)


def body(frames, live, norm_gain, w_qkv, w_out, cotangent):
    length = frames.shape[1]
    n_data = lax.axis_size("dp")
    n_seq = lax.axis_size("seq")
    full_qkv, full_out = (
        lax.all_gather(w_qkv, "dp", axis=0, tiled=True),
        lax.all_gather(w_out, "dp", axis=0, tiled=True),
    )
    inner = full_out.shape[0]
    heads = inner // HEAD_DIM
    hidden = frames[0].astype(jnp.float32)
    unit_rows, inverse = norm_rows(hidden)
    normed = (unit_rows * norm_gain).astype(jnp.bfloat16)
    projected = jnp.dot(normed, full_qkv, preferred_element_type=jnp.float32).astype(jnp.bfloat16)
    query = projected[:, :inner]
    key_values = projected[:, inner:]
    live_row = live[0]
    query_live = live_row.astype(jnp.float32)
    live_mark = live_row.astype(jnp.bfloat16)
    upstream = cotangent[0]
    grad_att = (against(upstream, full_out) * query_live[:, None]).astype(jnp.bfloat16)
    neighbours = -(-WIN // length)
    offsets = list(range(neighbours, 0, -1)) + list(range(-1, -neighbours - 1, -1))
    before_pairs, before_marks, after_pairs, after_marks = ([], [], [], [])
    for offset in offsets:
        distance = abs(offset)
        row_count = min(length, WIN - (distance - 1) * length)
        if offset > 0:
            send_pairs = key_values
            send_marks = live_mark
        else:
            send_pairs = key_values
            send_marks = live_mark
        got_pairs, got_marks = from_behind((send_pairs, send_marks), "seq", offset)
        if offset > 0:
            before_pairs.append(got_pairs)
            before_marks.append(got_marks)
        else:
            after_pairs.append(got_pairs)
            after_marks.append(got_marks)
    ext_pairs = jnp.concatenate(before_pairs + [key_values] + after_pairs, axis=0)
    ext_live = jnp.concatenate(before_marks + [live_mark] + after_marks, axis=0).astype(jnp.float32)
    total_span = length + 2 * WIN
    block_rows = min(length, 512)
    key_span = block_rows + 2 * WIN
    query_pos = jnp.arange(block_rows, dtype=jnp.int32)
    key_pos = jnp.arange(key_span, dtype=jnp.int32) - WIN
    in_window = jnp.abs(query_pos[:, None] - key_pos[None, :]) <= WIN
    allowances = [in_window & (ext_live[None, :] > 0.5)]
    score_scale = 1.0 / math.sqrt(HEAD_DIM)

    def split_heads(matrix):
        return matrix.reshape(matrix.shape[0], heads, HEAD_DIM).transpose(1, 0, 2)

    def merge_heads(matrix):
        return matrix.transpose(1, 0, 2).reshape(matrix.shape[1], inner)

    def one_head(inputs):
        query_head, key_head, value_head, grad_head = inputs
        out_blocks, query_blocks = ([], [])
        key_grads = jnp.zeros((total_span, HEAD_DIM), jnp.float32)
        value_grads = jnp.zeros((total_span, HEAD_DIM), jnp.float32)
        attended, grad_query, grad_key, grad_value = head_terms(
            query_head, key_head, value_head, grad_head, allowances[0], query_live, score_scale
        )
        out_blocks.append(attended)
        query_blocks.append(grad_query)
        key_grads = key_grads.at[0:key_span].add(grad_key)
        value_grads = value_grads.at[0:key_span].add(grad_value)
        return (
            jnp.concatenate(out_blocks, axis=0),
            jnp.concatenate(query_blocks, axis=0),
            key_grads,
            value_grads,
        )

    att_heads, query_heads, key_heads, value_heads = lax.map(
        one_head,
        (
            split_heads(query),
            split_heads(ext_pairs[:, :inner]),
            split_heads(ext_pairs[:, inner:]),
            split_heads(grad_att),
        ),
    )
    attention = merge_heads(att_heads)
    grad_query = merge_heads(query_heads)
    ext_grads = jnp.concatenate([merge_heads(key_heads), merge_heads(value_heads)], axis=1)
    own_grads = ext_grads[WIN : WIN + length]
    for offset in offsets:
        distance = abs(offset)
        row_count = min(length, WIN - (distance - 1) * length)
        if offset > 0:
            first_row = WIN - distance * length + length - row_count
        else:
            first_row = WIN + length + (distance - 1) * length
        arrived = from_behind(ext_grads[first_row : first_row + row_count], "seq", -offset)
        if offset > 0:
            own_grads = own_grads.at[length - row_count :].add(arrived)
        else:
            own_grads = own_grads.at[:row_count].add(arrived)
    grad_projected = jnp.concatenate([grad_query, own_grads], axis=1).astype(jnp.bfloat16)
    grad_unit = against(grad_projected, full_qkv) * norm_gain
    through = inverse * (
        grad_unit
        - jnp.mean(grad_unit, axis=-1, keepdims=True)
        - unit_rows * jnp.mean(grad_unit * unit_rows, axis=-1, keepdims=True)
    )
    grad_rows = (upstream.astype(jnp.float32) + through).astype(jnp.bfloat16)[None]
    factor = 1.0 / math.sqrt(n_data * n_seq * length)

    def blocked(left, right):
        left_tiles = left.reshape(length, n_data, left.shape[1] // n_data)
        right_tiles = right.reshape(length, n_seq, right.shape[1] // n_seq)
        tile_grid = jnp.einsum(
            "fpr,fsc->psrc", left_tiles, right_tiles, preferred_element_type=jnp.float32
        )
        return tile_grid.reshape(n_data * n_seq * left_tiles.shape[2], right_tiles.shape[2])

    sum_qkv, sum_out = (
        lax.psum_scatter(
            blocked(normed, grad_projected), ("dp", "seq"), scatter_dimension=0, tiled=True
        ),
        lax.psum_scatter(
            blocked(attention, upstream), ("dp", "seq"), scatter_dimension=0, tiled=True
        ),
    )
    return (grad_rows, sum_qkv * factor, sum_out * factor)


def swap(value, flip):
    count = lax.axis_size("seq")
    return lax.ppermute(value, "seq", [(source, source ^ flip) for source in range(count)])


def attend_kernel(score_scale, blocks, q_ref, g_ref, k_ref, v_ref, ends_ref, live_ref, qlive_ref,
                  att_ref, dq_ref, own_ref, other_ref, bias_ref):
    rows = q_ref.shape[1] // blocks
    span = k_ref.shape[1]

    @pl.when(pl.program_id(0) == 0)
    def _():
        for block in range(blocks):
            columns = slice(block * rows, (block + 1) * rows)
            near = jnp.abs(ends_ref[...] - qlive_ref[0:1, columns]) <= WIN
            bias_ref[:, columns] = jnp.where(near & (live_ref[...] > 0.5), 0.0, NEG)

    key_t, value_t = k_ref[...], v_ref[...]
    key = key_t.T
    value = value_t.T
    key_grad = jnp.zeros((span, HEAD_DIM), jnp.float32)
    value_grad = jnp.zeros((span, HEAD_DIM), jnp.float32)
    for block in range(blocks):
        columns = slice(block * rows, (block + 1) * rows)
        query_t, grad_t = q_ref[:, columns], g_ref[:, columns]
        scores = jnp.dot(
            key, (query_t * score_scale).astype(jnp.bfloat16), preferred_element_type=jnp.float32
        )
        scores = scores + bias_ref[:, columns]
        exponent = jnp.exp(scores - jnp.max(scores, axis=0, keepdims=True))
        inverse = 1.0 / jnp.sum(exponent, axis=0, keepdims=True)
        probabilities = exponent * inverse
        probs_b = probabilities.astype(jnp.bfloat16)
        mixed = jnp.dot(value_t, probs_b, preferred_element_type=jnp.float32)
        attended = (mixed * qlive_ref[1:2, columns]).astype(jnp.bfloat16)
        att_ref[:, columns] = attended
        row_delta = jnp.sum(
            grad_t.astype(jnp.float32) * attended.astype(jnp.float32), axis=0, keepdims=True
        )
        grad_probs = jnp.dot(
            value, (grad_t * score_scale).astype(jnp.bfloat16), preferred_element_type=jnp.float32
        )
        grad_scores = (probabilities * (grad_probs - row_delta * score_scale)).astype(
            jnp.bfloat16
        )
        dq_ref[:, columns] = jnp.dot(
            key_t, grad_scores, preferred_element_type=jnp.float32
        ).astype(jnp.bfloat16)
        key_grad += against(grad_scores, query_t)
        value_grad += against(probs_b, grad_t)
    half = span // 2
    key_grad_t, value_grad_t = key_grad.T, value_grad.T
    own_ref[0] = key_grad_t[:, :half]
    own_ref[1] = value_grad_t[:, :half]
    other_ref[0] = key_grad_t[:, half:].astype(jnp.bfloat16)
    other_ref[1] = value_grad_t[:, half:].astype(jnp.bfloat16)


def attend(query_t, grad_t, key_t, value_t, key_pos, key_live, query_rows, blocks, score_scale):
    features, queries = query_t.shape
    span = key_t.shape[1]
    half = span // 2
    heads = features // HEAD_DIM
    by_query = pl.BlockSpec((HEAD_DIM, queries), lambda h: (h, 0))
    by_key = pl.BlockSpec((HEAD_DIM, span), lambda h: (h, 0))
    grads = pl.BlockSpec((2, HEAD_DIM, half), lambda h: (0, h, 0))
    return pl.pallas_call(
        functools.partial(attend_kernel, score_scale, blocks),
        grid=(heads,),
        in_specs=[
            by_query,
            by_query,
            by_key,
            by_key,
            pl.BlockSpec((span, 1), lambda h: (0, 0)),
            pl.BlockSpec((span, 1), lambda h: (0, 0)),
            pl.BlockSpec((2, queries), lambda h: (0, 0)),
        ],
        out_specs=[by_query, by_query, grads, grads],
        out_shape=[
            jax.ShapeDtypeStruct((features, queries), jnp.bfloat16),
            jax.ShapeDtypeStruct((features, queries), jnp.bfloat16),
            jax.ShapeDtypeStruct((2, features, half), jnp.float32),
            jax.ShapeDtypeStruct((2, features, half), jnp.bfloat16),
        ],
        scratch_shapes=[pltpu.VMEM((span, queries), jnp.float32)],
        compiler_params=pltpu.CompilerParams(vmem_limit_bytes=40 * 2**20),
        cost_estimate=pl.CostEstimate(
            flops=10 * features * queries * span,
            bytes_accessed=12 * features * span,
            transcendentals=heads * queries * span,
        ),
    )(query_t, grad_t, key_t, value_t, key_pos, key_live, query_rows)


MESH = pl.DeviceIdType.MESH


def gather_kernel(piece_ref, out_ref, line_send, line_recv, side_send, side_recv,
                  core_send, core_recv, local_sem):
    count = out_ref.shape[0]
    dp, seq = lax.axis_index("dp"), lax.axis_index("seq")
    z, x, core = dp // 2, dp % 2, seq % 2
    mate = seq + 1 - 2 * core
    steps = 2 * count - 1
    above, below = z < count - 1, z > 0

    barrier = pltpu.get_barrier_semaphore()
    pl.semaphore_signal(barrier, inc=1, device_id={"dp": 2 * z + 1 - x}, device_id_type=MESH)
    pl.semaphore_signal(barrier, inc=1, device_id={"seq": mate}, device_id_type=MESH)

    @pl.when(above)
    def _():
        pl.semaphore_signal(barrier, inc=1, device_id={"dp": dp + 2}, device_id_type=MESH)

    @pl.when(below)
    def _():
        pl.semaphore_signal(barrier, inc=1, device_id={"dp": dp - 2}, device_id_type=MESH)

    pl.semaphore_wait(barrier, 2 + above.astype(jnp.int32) + below.astype(jnp.int32))

    def line(hop, up):
        origin = z - hop if up else z + hop
        source = piece_ref if hop == 0 else out_ref.at[origin, x, core]
        flow = 0 if up else 1
        return pltpu.make_async_remote_copy(
            src_ref=source, dst_ref=out_ref.at[origin, x, core],
            send_sem=line_send.at[flow, hop], recv_sem=line_recv.at[flow, hop],
            device_id={"dp": dp + 2 if up else dp - 2}, device_id_type=MESH,
        )

    def line_arrival(hop, up):
        origin = z - hop if up else z + hop
        flow = 0 if up else 1
        return pltpu.make_async_remote_copy(
            src_ref=piece_ref, dst_ref=out_ref.at[origin, x, core],
            send_sem=line_send.at[flow, hop - 1], recv_sem=line_recv.at[flow, hop - 1],
            device_id={"dp": dp + 2 if up else dp - 2}, device_id_type=MESH,
        )

    def side(step, origin, column):
        source = piece_ref if step == 0 else out_ref.at[origin, x, core]
        return pltpu.make_async_remote_copy(
            src_ref=source, dst_ref=out_ref.at[origin, column, core],
            send_sem=side_send.at[step], recv_sem=side_recv.at[step],
            device_id={"dp": 2 * z + 1 - x}, device_id_type=MESH,
        )

    def across(slot, origin, column, half):
        source = piece_ref if slot == 0 else out_ref.at[origin, column, core]
        return pltpu.make_async_remote_copy(
            src_ref=source, dst_ref=out_ref.at[origin, column, half],
            send_sem=core_send.at[slot], recv_sem=core_recv.at[slot],
            device_id={"seq": mate}, device_id_type=MESH,
        )

    waves = [(0, z, None)]
    for hop in range(1, count):
        waves.append((hop, z - hop, z >= hop))
        waves.append((count - 1 + hop, z + hop, z + hop < count))

    def guarded(condition, action):
        if condition is None:
            action()
        else:
            pl.when(condition)(action)

    keep = pltpu.make_async_copy(piece_ref, out_ref.at[z, x, core], local_sem)
    keep.start()
    pl.when(above)(lambda: line(0, True).start())
    pl.when(below)(lambda: line(0, False).start())
    side(0, z, x).start()
    across(0, z, x, core).start()

    def side_wave(step, origin):
        side(step, origin, 1 - x).wait_recv()
        across(steps + step, origin, 1 - x, core).start()

    for step, origin, condition in waves[1:]:
        up = step < count
        hop = step if up else step - count + 1

        def forward(step=step, origin=origin, up=up, hop=hop):
            line_arrival(hop, up).wait_recv()
            if hop < count - 1:
                pl.when(above if up else below)(lambda: line(hop, up).start())
            side(step, origin, x).start()
            across(step, origin, x, core).start()

        guarded(condition, forward)
        if not up:
            for late, place, holds in waves:
                late_hop = late if late < count else late - count + 1
                if late_hop == hop - 1:
                    guarded(holds, functools.partial(side_wave, late, place))
    for late, place, holds in waves[-2:]:
        guarded(holds, functools.partial(side_wave, late, place))

    keep.wait()
    for step, origin, condition in waves:
        def finish(step=step, origin=origin):
            side(step, origin, x).wait_send()
            across(step, origin, x, core).wait_send()
            across(steps + step, origin, 1 - x, core).wait_send()
            across(step, origin, x, 1 - core).wait_recv()
            across(steps + step, origin, 1 - x, 1 - core).wait_recv()
            up = step < count
            hop = step if up else step - count + 1
            if step == 0:
                pl.when(above)(lambda: line(0, True).wait_send())
                pl.when(below)(lambda: line(0, False).wait_send())
            elif hop < count - 1:
                pl.when(above if up else below)(lambda: line(hop, up).wait_send())

        guarded(condition, finish)


def gather_pieces(piece, count):
    steps = 2 * count - 1
    dma = pltpu.SemaphoreType.DMA
    return pl.pallas_call(
        gather_kernel,
        out_shape=jax.ShapeDtypeStruct((count, 2, 2) + piece.shape, piece.dtype),
        in_specs=[pl.BlockSpec(memory_space=pltpu.VMEM)],
        out_specs=pl.BlockSpec(memory_space=pltpu.VMEM),
        scratch_shapes=[
            dma((2, count)), dma((2, count)), dma((steps,)), dma((steps,)),
            dma((2 * steps,)), dma((2 * steps,)), dma(()),
        ],
        compiler_params=pltpu.CompilerParams(
            collective_id=0, has_side_effects=True, vmem_limit_bytes=24 * 2**20
        ),
        cost_estimate=pl.CostEstimate(
            flops=0, bytes_accessed=64 * piece.size * count, transcendentals=0
        ),
    )(piece)


def sum_kernel(chunks, factor, *refs):
    ins, outs = refs[:2], refs[2:4]
    beside, summed, lined = refs[4:6], refs[6:8], refs[8:10]
    side_send, side_recv, line_send, line_recv = refs[10:]
    count = ins[0].shape[0]
    dp = lax.axis_index("dp")
    z, x = dp // 2, dp % 2
    neighbour = 2 * z + 1 - x
    peers = [lax.rem(z + step, count) for step in range(1, count)]

    barrier = pltpu.get_barrier_semaphore()
    pl.semaphore_signal(barrier, inc=1, device_id={"dp": neighbour}, device_id_type=MESH)
    for peer in peers:
        pl.semaphore_signal(barrier, inc=1, device_id={"dp": 2 * peer + x}, device_id_type=MESH)
    pl.semaphore_wait(barrier, count)

    def rows_of(which, chunk):
        size = ins[which].shape[2] // chunks
        return pl.ds(chunk * size, size)

    def side(which, chunk):
        return pltpu.make_async_remote_copy(
            src_ref=ins[which].at[:, 1 - x, rows_of(which, chunk)],
            dst_ref=beside[which].at[chunk],
            send_sem=side_send.at[which, chunk], recv_sem=side_recv.at[which, chunk],
            device_id={"dp": neighbour}, device_id_type=MESH,
        )

    def line(which, chunk, step):
        peer = peers[step]
        return pltpu.make_async_remote_copy(
            src_ref=summed[which].at[chunk, peer],
            dst_ref=lined[which].at[chunk, step],
            send_sem=line_send.at[which, chunk, step], recv_sem=line_recv.at[which, chunk, step],
            device_id={"dp": 2 * peer + x}, device_id_type=MESH,
        )

    both = [(chunk, which) for chunk in range(chunks) for which in (0, 1)]
    for chunk, which in both:
        side(which, chunk).start()
    for chunk, which in both:
        side(which, chunk).wait_recv()
        for step in range(count - 1):
            peer = peers[step]
            summed[which][chunk, peer] = (
                ins[which][peer, x, rows_of(which, chunk)].astype(jnp.float32)
                + beside[which][chunk, peer].astype(jnp.float32)
            ).astype(jnp.bfloat16)
            line(which, chunk, step).start()
    for chunk, which in both:
        total = ins[which][z, x, rows_of(which, chunk)].astype(jnp.float32)
        total = total + beside[which][chunk, z].astype(jnp.float32)
        for step in range(count - 1):
            line(which, chunk, step).wait_recv()
            total = total + lined[which][chunk, step].astype(jnp.float32)
        outs[which][rows_of(which, chunk)] = total * factor
    for chunk, which in both:
        side(which, chunk).wait_send()
        for step in range(count - 1):
            line(which, chunk, step).wait_send()


def sum_tiles(arrays, count, chunks, factor):
    tiles = [a.reshape(count, 2, a.shape[0] // (2 * count), a.shape[1]) for a in arrays]
    vmem = pl.BlockSpec(memory_space=pltpu.VMEM)
    dma = pltpu.SemaphoreType.DMA

    def slots(lead):
        return [
            pltpu.VMEM((chunks, lead, t.shape[2] // chunks, t.shape[3]), t.dtype) for t in tiles
        ]

    return pl.pallas_call(
        functools.partial(sum_kernel, chunks, factor),
        out_shape=[jax.ShapeDtypeStruct(t.shape[2:], jnp.float32) for t in tiles],
        in_specs=[vmem, vmem],
        out_specs=[vmem, vmem],
        scratch_shapes=slots(count) + slots(count) + slots(count - 1) + [
            dma((2, chunks)), dma((2, chunks)),
            dma((2, chunks, count - 1)), dma((2, chunks, count - 1)),
        ],
        compiler_params=pltpu.CompilerParams(
            collective_id=1, has_side_effects=True, vmem_limit_bytes=24 * 2**20
        ),
        cost_estimate=pl.CostEstimate(
            flops=0, bytes_accessed=64 * tiles[0].size, transcendentals=0
        ),
    )(*tiles)


def assemble_kernel(two_ref, beside_ref, facing_ref, corner_ref, out_ref):
    low = lax.axis_index("seq") % 2
    queries = two_ref.shape[1]
    length, unit = queries // 2, facing_ref.shape[0]

    def place(two_row, one_row):
        out_ref[two_row : two_row + 2 * unit, :queries] = two_ref[...]
        out_ref[two_row : two_row + 2 * unit, queries:] = beside_ref[...]
        rows = slice(one_row, one_row + unit)
        for start, piece in ((0, facing_ref), (queries, corner_ref)):
            out_ref[rows, start : start + length] = piece[:, length:]
            out_ref[rows, start + length : start + queries] = piece[:, :length]

    pl.when(low == 0)(lambda: place(0, 2 * unit))
    pl.when(low == 1)(lambda: place(unit, 0))


def assemble(two, beside, facing, corner):
    vmem = pl.BlockSpec(memory_space=pltpu.VMEM)
    rows, queries = two.shape
    return pl.pallas_call(
        assemble_kernel,
        out_shape=jax.ShapeDtypeStruct((rows + facing.shape[0], 2 * queries), two.dtype),
        in_specs=[vmem] * 4,
        out_specs=vmem,
        compiler_params=pltpu.CompilerParams(vmem_limit_bytes=16 * 2**20),
        cost_estimate=pl.CostEstimate(flops=0, bytes_accessed=8 * two.size, transcendentals=0),
    )(two, beside, facing, corner)


def head_body(frames, live, norm_gain, w_qkv, w_out, cotangent):
    length, width = frames.shape[1:]
    n_data = lax.axis_size("dp")
    n_seq = lax.axis_size("seq")
    me = lax.axis_index("seq")
    high, low = me // 2, me % 2
    shard = w_qkv.shape[0]
    inner = w_qkv.shape[1] // 3
    part = inner // 2
    score_scale = 1.0 / math.sqrt(HEAD_DIM)

    own_rows = lax.dynamic_slice_in_dim(w_qkv, low * (shard // 2), shard // 2, 0)
    choices = [
        jnp.concatenate(
            [own_rows[:, (2 * i + half) * part : (2 * i + half + 1) * part] for i in range(3)],
            axis=1,
        )
        for half in (0, 1)
    ]
    mine_qkv = jnp.where(high == 0, choices[0], choices[1])
    mine_out = lax.dynamic_slice_in_dim(w_out, low * (width // 2), width // 2, 1)
    packed_weights = jnp.concatenate([mine_out, mine_qkv], axis=1)

    upstream = cotangent[0]
    marks = live.astype(jnp.float32)
    packs = [frames[0]] + [swap(frames[0], flip) for flip in (2, 1, 3)]
    cots = jnp.concatenate([upstream, swap(upstream, 2)], axis=0)
    rows = jnp.concatenate(packs, axis=0)
    key_live = jnp.concatenate([marks] + [swap(marks, flip) for flip in (2, 1, 3)], axis=1)[0]
    step = jnp.arange(length, dtype=jnp.float32)
    key_pos = jnp.concatenate(
        [step + ((me ^ flip) * length).astype(jnp.float32) for flip in (0, 2, 1, 3)]
    )
    queries = 2 * length
    query_live = key_live[:queries]

    unit_rows, inverse = norm_rows(rows.astype(jnp.float32))
    normed = (unit_rows * norm_gain).astype(jnp.bfloat16)

    gathered = gather_pieces(packed_weights, n_data // 2)
    part_qkv = gathered[..., width // 2 :].reshape(n_data * shard, 3 * part)
    halves = gathered[..., : width // 2].reshape(n_data, 2, shard // 2, width // 2)
    halves = lax.dynamic_slice_in_dim(halves, high * (n_data // 2), n_data // 2, 0)
    part_out = jnp.concatenate(
        [halves[:, half].reshape(part, width // 2) for half in (0, 1)], axis=1
    )

    def turned(weights, values):
        return lax.dot_general(
            weights, values, (((0,), (1,)), ((), ())), preferred_element_type=jnp.float32
        )

    query_t = turned(part_qkv[:, :part], normed[:queries]).astype(jnp.bfloat16)
    pairs_t = turned(part_qkv[:, part:], normed).astype(jnp.bfloat16)
    grad_t = (against(part_out, cots) * query_live[None, :]).astype(jnp.bfloat16)

    query_rows = jnp.stack([key_pos[:queries], query_live])
    att_t, dq_t, own_grads, other_grads = attend(
        query_t, grad_t, pairs_t[:part], pairs_t[part:],
        key_pos[:, None], key_live[:, None], query_rows, 2, score_scale,
    )
    block = width // n_seq
    other_grads = swap(other_grads, 1)
    partial_out = jnp.dot(att_t, cots, preferred_element_type=jnp.float32)
    other_grads, partial_out = lax.optimization_barrier((other_grads, partial_out))
    own_grads = own_grads + other_grads.astype(jnp.float32)

    grads_t = jnp.concatenate(
        [dq_t, own_grads.reshape(2 * part, queries).astype(jnp.bfloat16)], axis=0
    )
    unit = part // 2

    def units(start, count):
        return lax.dynamic_slice_in_dim(grads_t, start * unit, count * unit, 0)

    beside = swap(units(2 * (high + 1 - low), 2), 1)
    facing = swap(units(4 * (1 - high) + low, 1), 2)
    corner = swap(units(4 * (1 - high) + 1 - low, 1), 3)

    def columns_of(flip):
        return lax.dynamic_slice_in_dim(partial_out, (me ^ flip) * block, block, 1)

    blocks = [columns_of(flip).astype(jnp.bfloat16) for flip in (1, 2, 3)]
    blocks, facing, corner = lax.optimization_barrier((blocks, facing, corner))
    columns = [swap(value, flip) for value, flip in zip(blocks, (1, 2, 3))]
    keep_t = assemble(units(2 * (high + low), 2), beside, facing, corner)
    late_t, columns = lax.optimization_barrier((grads_t, columns))
    sum_qkv = lax.dot_general(
        normed, keep_t, (((0,), (1,)), ((), ())), preferred_element_type=jnp.float32
    )

    columns = [value.astype(jnp.float32) for value in columns]
    same, across = columns_of(0) + columns[0], columns[1] + columns[2]
    sum_out = jnp.concatenate(
        [jnp.where(high == 0, same, across), jnp.where(high == 0, across, same)], axis=0
    )

    def through_weights(piece):
        return lax.dot_general(
            piece, part_qkv, (((0,), (1,)), ((), ())), preferred_element_type=jnp.float32
        )

    sent = through_weights(late_t[:, length:]).astype(jnp.bfloat16)
    sent, sum_qkv = lax.optimization_barrier((sent, sum_qkv.astype(jnp.bfloat16)))
    arrived = swap(sent, 2)
    factor = 1.0 / math.sqrt(n_data * n_seq * length)
    tile_qkv, tile_out = sum_tiles(
        [sum_qkv, sum_out.astype(jnp.bfloat16)], n_data // 2, 5, factor
    )
    grad_unit = through_weights(late_t[:, :length]) + arrived.astype(jnp.float32)
    grad_unit = grad_unit * norm_gain
    own_unit = unit_rows[:length]
    through = inverse[:length] * (
        grad_unit
        - jnp.mean(grad_unit, axis=-1, keepdims=True)
        - own_unit * jnp.mean(grad_unit * own_unit, axis=-1, keepdims=True)
    )
    grad_rows = (upstream.astype(jnp.float32) + through).astype(jnp.bfloat16)[None]

    return (grad_rows, tile_qkv, tile_out)


def solution(mesh):
    n_seq = mesh.shape["seq"]

    def whole(frames, live, norm_gain, w_qkv, w_out, cotangent):
        heads_fit = n_seq == 4 and mesh.shape["dp"] == 8 and frames.shape[1] <= frames.shape[1] // n_seq + 2 * WIN
        chosen = head_body if heads_fit else body
        return split(chosen, mesh)(frames, live, norm_gain, w_qkv, w_out, cotangent)

    return whole


def split(chosen, mesh):
    return jax.shard_map(
        chosen,
        mesh=mesh,
        in_specs=(
            P("dp", "seq", None),
            P("dp", "seq"),
            P(),
            P("dp", None),
            P("dp", None),
            P("dp", "seq", None),
        ),
        out_specs=(P("dp", "seq", None), P("dp", "seq"), P("dp", "seq")),
        check_vma=False,
    )
```
